32 devices in a mesh: dp: 16 (over z, y, core), hst: 2 (over x).
Axes of the slice: x: 2, y: 2, z: 4, core: 2. Of those that a mesh axis runs over, the one named last changes fastest.
Arguments:
- image_embeds: float32 [16, 2, 256, 1024], P('dp', 'hst'), may hold values from -16 to 16
- text_embeds: float32 [16, 2, 256, 1024], P('dp', 'hst'), may hold values from -16 to 16
Outputs:
- mean_loss: float32 [], replicated
- image_grads: float32 [16, 2, 256, 1024], P('dp', 'hst')
- text_grads: float32 [16, 2, 256, 1024], P('dp', 'hst')
The draws below stay inside these ranges and needn't reach their ends.
All inputs are finite; a program needn't handle non-finite values.
Results may differ from the reference program's by a relative error of at most 0.000068.
Values sent between devices are 32-bit elements; how exact they have to be, the bound alone decides.
No kernel may reach another device: no remote copies, remote signals or barrier semaphores. Data moves between devices by JAX's collectives and lax.ppermute only.
A program may use at most 64 MiB of HBM per device.

```python
import jax
import jax.numpy as jnp
from jax import lax

D = 1024
ROWS = 256
CYCLE = 16
GROUPS = 2


def pair_shape():
    return (CYCLE, GROUPS, ROWS, D)


def drawn_rows(key):
    base_key, level_key, spot_key = jax.random.split(jax.random.fold_in(key, 101), 3)
    shared_base = jnp.clip(jax.random.normal(base_key, pair_shape(), jnp.float32), -4.0, 4.0)
    levels = jnp.array([2.9, 3.3, 3.8], jnp.float32)
    strength = levels[jax.random.randint(level_key, (CYCLE, GROUPS, 1, 1), 0, 3)]
    chosen_row = 2 * jax.random.randint(spot_key, (CYCLE, GROUPS, 1, 1), 0, ROWS // 2)
    row_index = lax.broadcasted_iota(jnp.int32, (1, 1, ROWS, 1), 2)
    return (shared_base, strength, row_index == chosen_row, row_index == chosen_row + 1)


def shared_parts(key):
    pair_key = jax.random.fold_in(key, 103)
    normal_pair = jnp.clip(jax.random.normal(pair_key, pair_shape(), jnp.float32), -6.0, 6.0)
    return normal_pair


def alignment(top_share):
    block_index = lax.broadcasted_iota(jnp.int32, (CYCLE, GROUPS, 1, 1), 0) * GROUPS + lax.broadcasted_iota(jnp.int32, (CYCLE, GROUPS, 1, 1), 1)
    fraction = block_index.astype(jnp.float32) / max(CYCLE * GROUPS - 1, 1)
    return top_share * (1.0 - fraction)


def row_spread(key):
    return jnp.exp(jax.random.uniform(key, (CYCLE, GROUPS, ROWS, 1), jnp.float32, jnp.log(0.8), jnp.log(1.6)))


def place_aligned(key, values, shared):
    shared_base, strength, first_rows, second_rows = shared
    closeness = 1.0 - 1.0 / (16.0 * strength * strength)
    offset = 0.03 * jnp.clip(jax.random.normal(key, pair_shape(), jnp.float32), -4.0, 4.0)
    return jnp.where(first_rows, strength * shared_base, jnp.where(second_rows, strength * (closeness * shared_base + offset), values))


def draw_image_embeds(key, part):
    shared = drawn_rows(key)
    normal_pair = shared_parts(key)
    key = jax.random.fold_in(key, 1)
    scale_key, offset_key = jax.random.split(key, 2)
    values = normal_pair
    values = values * row_spread(scale_key)
    return place_aligned(offset_key, values, shared)


def draw_text_embeds(key, part):
    shared = drawn_rows(key)
    normal_pair = shared_parts(key)
    key = jax.random.fold_in(key, 2)
    scale_key, offset_key, own_key = jax.random.split(key, 3)
    own = jnp.clip(jax.random.normal(own_key, pair_shape(), jnp.float32), -6.0, 6.0)
    share = alignment(0.15)
    values = share * normal_pair + jnp.sqrt(1.0 - share * share) * own
    values = values * row_spread(scale_key)
    return place_aligned(offset_key, values, shared)


def setup_inputs(seed: int = 0) -> dict:
    arg_keys = jax.random.split(jax.random.key(seed), 3)
    image_embeds = draw_image_embeds(jax.random.fold_in(arg_keys[2], 71), 0)
    text_embeds = draw_text_embeds(jax.random.fold_in(arg_keys[2], 71), 0)
    return {"image_embeds": image_embeds, "text_embeds": text_embeds}


logit_scale = 0.03125
highest = lax.Precision.HIGHEST


def block_logits(left_side, right_side):
    return logit_scale * jnp.einsum("dhrk,dhsk->dhrs", left_side, right_side, precision=highest)


def reference(image_embeds, text_embeds):
    earlier_texts = jnp.roll(text_embeds, 1, axis=0)
    self_logits = block_logits(image_embeds, text_embeds)
    earlier_logits = block_logits(image_embeds, earlier_texts)
    row_logsum = jax.nn.logsumexp(jnp.concatenate([self_logits, earlier_logits], axis=3), axis=3)
    later_logits = jnp.roll(earlier_logits, -1, axis=0)
    column_logsum = jax.nn.logsumexp(jnp.concatenate([self_logits, later_logits], axis=2), axis=2)
    positive = jnp.diagonal(self_logits, axis1=2, axis2=3)
    loss_total = 0.5 * (jnp.sum(row_logsum) + jnp.sum(column_logsum)) - jnp.sum(positive)
    mean_loss = loss_total / (CYCLE * GROUPS * ROWS)
    before_logsum = jnp.roll(column_logsum, 1, axis=0)
    identity = jnp.eye(ROWS, dtype=jnp.float32)
    self_weights = 0.5 * (jnp.exp(self_logits - row_logsum[..., None]) + jnp.exp(self_logits - column_logsum[:, :, None, :])) - identity
    earlier_weights = 0.5 * (jnp.exp(earlier_logits - row_logsum[..., None]) + jnp.exp(earlier_logits - before_logsum[:, :, None, :]))
    image_sum = jnp.einsum("dhrs,dhsk->dhrk", self_weights, text_embeds, precision=highest) + jnp.einsum("dhrs,dhsk->dhrk", earlier_weights, earlier_texts, precision=highest)
    earlier_grads = jnp.einsum("dhrs,dhrk->dhsk", earlier_weights, image_embeds, precision=highest)
    text_sum = jnp.einsum("dhrs,dhrk->dhsk", self_weights, image_embeds, precision=highest) + jnp.roll(earlier_grads, -1, axis=0)
    return mean_loss, logit_scale * image_sum, logit_scale * text_sum
```

```python
import jax
import jax.numpy as jnp
from jax import lax
from jax.experimental import pallas as pl
from jax.experimental.pallas import tpu as pltpu
from jax.sharding import PartitionSpec as P

logit_scale = 0.03125
f32, bf16 = jnp.float32, jnp.bfloat16
LANES = 128


def from_behind(value, axis, steps):
    count = lax.axis_size(axis)
    pairs = [(source, (source + steps) % count) for source in range(count)]
    return lax.ppermute(value, axis, pairs)


def split(value):
    high = value.astype(bf16)
    rest = value - high.astype(f32)
    middle = rest.astype(bf16)
    low = (rest - middle.astype(f32)).astype(bf16)
    return high, middle, low


PAIRS = ((2, 0), (1, 1), (0, 2), (1, 0), (0, 1), (0, 0))


def rows_by_rows(left, right):
    return lax.dot_general(
        jnp.concatenate([left[one] for one, _ in PAIRS], axis=1),
        jnp.concatenate([right[other] for _, other in PAIRS], axis=1),
        (((1,), (1,)), ((), ())),
        preferred_element_type=f32,
    )


def left_parts(left):
    parts = split(left)
    return jnp.concatenate([parts[one] for one, _ in PAIRS], axis=1)


def rows_by_columns(left, right):
    return jnp.dot(left, jnp.concatenate([right[other] for _, other in PAIRS], axis=0), preferred_element_type=f32)


def store_parts(stacked, value):
    for place, part in enumerate(split(value)):
        stacked[place] = part


def logsum(logits, axis):
    largest = jnp.max(logits, axis=axis, keepdims=True)
    return largest + jnp.log(jnp.sum(jnp.exp(logits - largest), axis=axis, keepdims=True))


def paired_logsum(former, latter):
    largest = jnp.maximum(former, latter)
    return largest + jnp.log(jnp.exp(former - largest) + jnp.exp(latter - largest))


def diagonal_mask(count):
    shape = (count, count)
    return lax.broadcasted_iota(jnp.int32, shape, 0) == lax.broadcasted_iota(jnp.int32, shape, 1)


def as_row(column, diagonal):
    return jnp.sum(jnp.where(diagonal, column, 0.0), axis=0, keepdims=True)


def as_column(row, diagonal):
    return jnp.sum(jnp.where(diagonal, row, 0.0), axis=1, keepdims=True)


def total(values):
    return jnp.sum(jnp.sum(values, axis=1, keepdims=True), axis=0, keepdims=True)


def unpack(message, place, count):
    rows = count // LANES
    return jnp.concatenate([message[place * rows + k : place * rows + k + 1, :] for k in range(rows)], axis=1)


def start(pairs, semaphores):
    copies = [pltpu.make_async_copy(source, target, semaphores.at[k]) for k, (source, target) in enumerate(pairs)]
    for copy in copies:
        copy.start()
    return copies


def self_kernel(
    images, texts,
    logits, image_parts, text_parts, row_part, positive, column_part, text_store,
    image_in, text_in, semaphores,
):
    copies = start([(images, image_in), (texts, text_in)], semaphores)
    copies[0].wait()
    store_parts(image_parts, image_in[...])
    copies[1].wait()
    store_parts(text_parts, text_in[...])
    copies = start([(text_parts, text_store)], semaphores.at[2:3])
    block = logit_scale * rows_by_rows(image_parts, text_parts)
    diagonal = diagonal_mask(block.shape[0])
    logits[...] = block
    row_part[...] = as_row(logsum(block, 1), diagonal)
    column_part[...] = logsum(block, 0)
    positive[...] = total(jnp.where(diagonal, block, 0.0))
    copies[0].wait()


def earlier_kernel(
    image_parts, text_parts, earlier_texts, logits, self_rows, self_columns, before_columns, positive,
    messages, image_part, row_term, column_term,
    earlier_parts, image_out, row_out, column_out, semaphores,
):
    store_parts(earlier_parts, earlier_texts[...])
    block = logit_scale * rows_by_rows(image_parts, earlier_parts)
    count, width = image_out.shape
    diagonal = diagonal_mask(count)
    own = logits[...]
    rows = paired_logsum(as_column(self_rows[...], diagonal), logsum(block, 1))
    columns = paired_logsum(before_columns[...], logsum(block, 0))
    messages[...] = jnp.broadcast_to(0.5 * (total(rows) + total(columns)) - positive[...], messages.shape)
    by_rows = 0.5 * jnp.exp(own - rows) - jnp.where(diagonal, 1.0, 0.0)
    by_columns = 0.5 * jnp.exp(own - self_columns[...])
    earlier_left = left_parts(0.5 * (jnp.exp(block - rows) + jnp.exp(block - columns)))
    row_left, row_down, column_down = left_parts(by_rows), left_parts(by_rows.T), left_parts(by_columns.T)
    half = width // 2
    outs = []
    for k in range(2):
        part = slice(k * half, (k + 1) * half)
        row_out[:, part] = rows_by_columns(row_down, image_parts.at[:, :, part])
        column_out[:, part] = rows_by_columns(column_down, image_parts.at[:, :, part])
        image_out[:, part] = rows_by_columns(earlier_left, earlier_parts.at[:, :, part]) + rows_by_columns(
            row_left, text_parts.at[:, :, part]
        )
        outs += start(
            [
                (source.at[:, part], target.at[:, part])
                for source, target in ((row_out, row_term), (column_out, column_term), (image_out, image_part))
            ],
            semaphores.at[3 * k : 3 * k + 3],
        )
    for copy in outs:
        copy.wait()


def image_kernel(
    text_store, later_images, logits, later_rows, self_columns, image_part,
    left, later_parts, columns_out, image_grads,
    text_parts, part_in, image_out, semaphores,
):
    copies = start([(text_store, text_parts), (image_part, part_in)], semaphores)
    count, width = image_out.shape
    diagonal = diagonal_mask(count)
    store_parts(later_parts, later_images[...])
    copies[0].wait()
    block = logit_scale * rows_by_rows(text_parts, later_parts)
    rows = paired_logsum(later_rows[...], logsum(block, 0))
    columns = paired_logsum(as_column(self_columns[...], diagonal), logsum(block, 1))
    left[...] = left_parts(0.5 * (jnp.exp(block - rows) + jnp.exp(block - columns)))
    across = as_row(columns, diagonal)
    columns_out[...] = across
    own_left = left_parts(0.5 * jnp.exp(logits[...] - across))
    copies[1].wait()
    outs = []
    half = width // 2
    for k in range(2):
        part = slice(k * half, (k + 1) * half)
        image_out[:, part] = logit_scale * (part_in[:, part] + rows_by_columns(own_left, text_parts.at[:, :, part]))
        outs += start([(image_out.at[:, part], image_grads.at[:, part])], semaphores.at[2 + k : 3 + k])
    for copy in outs:
        copy.wait()


def text_kernel(
    left, later_parts, columns, self_columns, row_term, column_term, messages,
    mean_loss, text_grads,
    row_in, column_in, text_out, semaphores,
):
    copies = start([(row_term, row_in), (column_term, column_in)], semaphores)
    count, width = text_out.shape
    mean_loss[...] = total(messages[:, 0, 0:1]) / (count * messages.shape[0])
    scale = as_column(jnp.exp(self_columns[...] - columns[...]), diagonal_mask(count))
    for copy in copies:
        copy.wait()
    outs = []
    half = width // 2
    for k in range(2):
        part = slice(k * half, (k + 1) * half)
        terms = rows_by_columns(left[...], later_parts.at[:, :, part])
        text_out[:, part] = logit_scale * (row_in[:, part] + scale * column_in[:, part] + terms)
        outs += start([(text_out.at[:, part], text_grads.at[:, part])], semaphores.at[2 + k : 3 + k])
    for copy in outs:
        copy.wait()


VM, HB, SM = pl.BlockSpec(memory_space=pltpu.VMEM), pl.BlockSpec(memory_space=pltpu.HBM), pl.BlockSpec(memory_space=pltpu.SMEM)


def call(kernel, products, ins, outs, scratch, copies):
    def shape_of(place, shape, dtype):
        if place is HB:
            return pltpu.HBM(shape, dtype)
        return jax.ShapeDtypeStruct(shape, dtype)

    run = pl.pallas_call(
        kernel,
        out_shape=[shape_of(*out) for out in outs],
        in_specs=ins,
        out_specs=[out[0] for out in outs],
        scratch_shapes=[pltpu.VMEM(shape, dtype) for shape, dtype in scratch]
        + ([pltpu.SemaphoreType.DMA((copies,))] if copies else []),
        compiler_params=pltpu.CompilerParams(vmem_limit_bytes=24 << 20),
        cost_estimate=pl.CostEstimate(
            flops=products * 12 * 256 * 256 * 1024, bytes_accessed=4 << 20, transcendentals=1 << 18
        ),
    )

    def pinned(*values):
        return run(
            *[pltpu.with_memory_space_constraint(v, pltpu.HBM) if spec is HB else v for v, spec in zip(values, ins)]
        )

    return pinned


def on_device(image_embeds, text_embeds):
    images, texts = image_embeds[0, 0], text_embeds[0, 0]
    count, width = images.shape
    square, row, whole = (count, count), (1, count), (count, width)
    parts, left = ((3, count, width), bf16), ((count, len(PAIRS) * count), bf16)
    devices = lax.axis_size("dp") * lax.axis_size("hst")
    earlier_texts = from_behind(texts, "dp", 1)
    logits, image_parts, text_parts, self_rows, positive, self_columns, text_store = call(
        self_kernel,
        1,
        [HB, HB],
        [(VM, square, f32), (VM, *parts), (VM, *parts), (VM, row, f32), (VM, (1, 1), f32), (VM, row, f32), (HB, *parts)],
        [(whole, f32), (whole, f32)],
        3,
    )(images, texts)
    before_columns = from_behind(self_columns, "dp", 1)
    later_rows = from_behind(self_rows, "dp", -1)
    earlier_texts, images, before_columns, later_rows = lax.optimization_barrier(
        (earlier_texts, images, before_columns, later_rows)
    )
    later_images = from_behind(images, "dp", -1)
    messages, image_part, row_term, column_term = call(
        earlier_kernel,
        5,
        [VM] * 8,
        [(VM, (devices, 1, LANES), f32)] + [(HB, whole, f32)] * 3,
        [parts] + [(whole, f32)] * 3,
        6,
    )(image_parts, text_parts, earlier_texts, logits, self_rows, self_columns, before_columns, positive)
    messages = lax.all_to_all(messages, ("dp", "hst"), 0, 0, tiled=True)
    left, later_parts, columns, image_grads = call(
        image_kernel,
        2,
        [HB, VM, VM, VM, VM, HB],
        [(VM, *left), (VM, *parts), (VM, row, f32), (HB, whole, f32)],
        [parts, (whole, f32), (whole, f32)],
        4,
    )(text_store, later_images, logits, later_rows, self_columns, image_part)
    mean_loss, text_grads = call(
        text_kernel,
        1,
        [VM] * 4 + [HB, HB, VM],
        [(VM, (1, 1), f32), (HB, whole, f32)],
        [(whole, f32)] * 3,
        4,
    )(left, later_parts, columns, self_columns, row_term, column_term, messages)
    return mean_loss[0, 0], image_grads[None, None], text_grads[None, None]


def solution(mesh):
    return jax.shard_map(
        on_device,
        mesh=mesh,
        in_specs=(P("dp", "hst", None, None), P("dp", "hst", None, None)),
        out_specs=(P(), P("dp", "hst", None, None), P("dp", "hst", None, None)),
        check_vma=False,
    )
```

```python
import functools

import jax
import jax.numpy as jnp
from jax import lax
from jax.experimental import pallas as pl
from jax.experimental.pallas import tpu as pltpu
from jax.sharding import PartitionSpec as P

logit_scale = 0.03125
f32, bf16 = jnp.float32, jnp.bfloat16
LANES = 128


def from_behind(value, axis, steps):
    count = lax.axis_size(axis)
    pairs = [(source, (source + steps) % count) for source in range(count)]
    return lax.ppermute(value, axis, pairs)


def split(value):
    high = value.astype(bf16)
    rest = value - high.astype(f32)
    middle = rest.astype(bf16)
    low = (rest - middle.astype(f32)).astype(bf16)
    return high, middle, low


PAIRS = ((2, 0), (1, 1), (0, 2), (1, 0), (0, 1), (0, 0))


def rows_by_rows(left, right):
    return lax.dot_general(
        jnp.concatenate([left[one] for one, _ in PAIRS], axis=1),
        jnp.concatenate([right[other] for _, other in PAIRS], axis=1),
        (((1,), (1,)), ((), ())),
        preferred_element_type=f32,
    )


def left_parts(left):
    parts = split(left)
    return jnp.concatenate([parts[one] for one, _ in PAIRS], axis=1)


def rows_by_columns(left, right):
    return jnp.dot(left, jnp.concatenate([right[other] for _, other in PAIRS], axis=0), preferred_element_type=f32)


def store_parts(stacked, value):
    for place, part in enumerate(split(value)):
        stacked[place] = part


def logsum(logits, axis):
    largest = jnp.max(logits, axis=axis, keepdims=True)
    return largest + jnp.log(jnp.sum(jnp.exp(logits - largest), axis=axis, keepdims=True))


def paired_logsum(former, latter):
    largest = jnp.maximum(former, latter)
    return largest + jnp.log(jnp.exp(former - largest) + jnp.exp(latter - largest))


def diagonal_mask(count):
    shape = (count, count)
    return lax.broadcasted_iota(jnp.int32, shape, 0) == lax.broadcasted_iota(jnp.int32, shape, 1)


def as_row(column, diagonal):
    return jnp.sum(jnp.where(diagonal, column, 0.0), axis=0, keepdims=True)


def as_column(row, diagonal):
    return jnp.sum(jnp.where(diagonal, row, 0.0), axis=1, keepdims=True)


def total(values):
    return jnp.sum(jnp.sum(values, axis=1, keepdims=True), axis=0, keepdims=True)


def start(pairs, semaphores):
    copies = [pltpu.make_async_copy(source, target, semaphores.at[k]) for k, (source, target) in enumerate(pairs)]
    for copy in copies:
        copy.start()
    return copies


def columns_at(k, size):
    return pl.ds(pl.multiple_of(k * size, size), size)


def self_kernel(
    images, texts,
    logits, image_parts, row_part, positive, column_part, image_store, text_store, row_product, column_term,
    image_in, text_in, text_parts, left, down, row_out, column_out, semaphores,
):
    copies = start([(images, image_in), (texts, text_in)], semaphores)
    copies[0].wait()
    store_parts(image_parts, image_in[...])
    copies[1].wait()
    store_parts(text_parts, text_in[...])
    copies = start([(image_parts, image_store), (text_parts, text_store)], semaphores)
    block = logit_scale * rows_by_rows(image_parts, text_parts)
    count, width = text_in.shape
    diagonal = diagonal_mask(count)
    rows, columns = logsum(block, 1), logsum(block, 0)
    logits[...] = block
    row_part[...] = as_row(rows, diagonal)
    column_part[...] = columns
    positive[...] = total(jnp.where(diagonal, block, 0.0))
    left[...] = left_parts(0.5 * jnp.exp(block - rows))
    down[...] = left_parts((0.5 * jnp.exp(block - columns)).T)
    half = width // 2

    @pl.loop(0, 2)
    def _(k):
        part = columns_at(k, half)
        row_out[:, part] = rows_by_columns(left[...], text_parts.at[:, :, part])
        column_out[:, part] = rows_by_columns(down[...], image_parts.at[:, :, part])

    copies += start([(row_out, row_product), (column_out, column_term)], semaphores.at[2:4])
    for copy in copies:
        copy.wait()


def earlier_kernel(
    image_parts, earlier_texts, self_rows, before_columns, positive,
    messages, weights, rows_out,
):
    block = logit_scale * rows_by_rows(image_parts, split(earlier_texts[...]))
    diagonal = diagonal_mask(block.shape[0])
    rows = paired_logsum(as_column(self_rows[...], diagonal), logsum(block, 1))
    columns = paired_logsum(before_columns[...], logsum(block, 0))
    messages[...] = jnp.broadcast_to(0.5 * (total(rows) + total(columns)) - positive[...], messages.shape)
    weights[...] = 0.5 * (jnp.exp(block - rows) + jnp.exp(block - columns))
    rows_out[...] = as_row(rows, diagonal)


def middle_kernel(
    weights, earlier_texts, rows, logits, self_rows, image_store, text_store, row_store,
    image_part, row_term, text_parts,
    earlier_parts, image_parts, row_product, left, down, semaphores,
):
    copies = start([(text_store, text_parts), (row_store, row_product), (image_store, image_parts)], semaphores)
    count, width = image_part.shape
    diagonal = diagonal_mask(count)
    left[...] = left_parts(weights[...])
    store_parts(earlier_parts, earlier_texts[...])
    joint = as_column(rows[...], diagonal)
    down[...] = left_parts((0.5 * jnp.exp(logits[...] - joint) - jnp.where(diagonal, 1.0, 0.0)).T)
    scale = as_column(jnp.exp(self_rows[...] - rows[...]), diagonal)
    half = width // 2
    copies[0].wait()
    copies[1].wait()

    @pl.loop(0, 2)
    def _(k):
        part = columns_at(k, half)
        own = text_parts[0, :, part].astype(f32) + text_parts[1, :, part].astype(f32) + text_parts[2, :, part].astype(f32)
        terms = rows_by_columns(left[...], earlier_parts.at[:, :, part])
        image_part[:, part] = terms + scale * row_product[:, part] - own

    copies[2].wait()

    @pl.loop(0, 2)
    def _(k):
        part = columns_at(k, half)
        row_term[:, part] = rows_by_columns(down[...], image_parts.at[:, :, part])


def last_kernel(
    text_parts, later_images, logits, later_rows, self_columns, image_part, row_term, column_term,
    image_grads, text_grads,
    later_parts, left, own_left, column_in, image_out, text_out, semaphores,
):
    (column_copy,) = start([(column_term, column_in)], semaphores.at[4:5])
    count, width = image_out.shape
    diagonal = diagonal_mask(count)
    store_parts(later_parts, later_images[...])
    block = logit_scale * rows_by_rows(text_parts, later_parts)
    rows = paired_logsum(later_rows[...], logsum(block, 0))
    own_columns = as_column(self_columns[...], diagonal)
    columns = paired_logsum(own_columns, logsum(block, 1))
    left[...] = left_parts(0.5 * (jnp.exp(block - rows) + jnp.exp(block - columns)))
    own_left[...] = left_parts(0.5 * jnp.exp(logits[...] - as_row(columns, diagonal)))
    scale = jnp.exp(own_columns - columns)
    half = width // 2
    column_copy.wait()

    def copies(k):
        part = columns_at(k, half)
        return (
            pltpu.make_async_copy(image_out.at[:, part], image_grads.at[:, part], semaphores.at[2 * k]),
            pltpu.make_async_copy(text_out.at[:, part], text_grads.at[:, part], semaphores.at[2 * k + 1]),
        )

    @pl.loop(0, 2)
    def _(k):
        part = columns_at(k, half)
        of_image, of_text = copies(k)
        terms = rows_by_columns(own_left[...], text_parts.at[:, :, part])
        image_out[:, part] = logit_scale * (image_part[:, part] + terms)
        of_image.start()
        terms = rows_by_columns(left[...], later_parts.at[:, :, part])
        text_out[:, part] = logit_scale * (row_term[:, part] + scale * column_in[:, part] + terms)
        of_text.start()

    for k in range(2):
        for copy in copies(k):
            copy.wait()


def loss_kernel(messages, mean_loss, *, rows):
    mean_loss[...] = total(messages[:, 0, 0:1]) / rows


VM, HB, SM = pl.BlockSpec(memory_space=pltpu.VMEM), pl.BlockSpec(memory_space=pltpu.HBM), pl.BlockSpec(memory_space=pltpu.SMEM)


def call(kernel, products, ins, outs, scratch, copies):
    def shape_of(place, shape, dtype):
        if place is HB:
            return pltpu.HBM(shape, dtype)
        return jax.ShapeDtypeStruct(shape, dtype)

    run = pl.pallas_call(
        kernel,
        out_shape=[shape_of(*out) for out in outs],
        in_specs=ins,
        out_specs=[out[0] for out in outs],
        scratch_shapes=[pltpu.VMEM(shape, dtype) for shape, dtype in scratch]
        + ([pltpu.SemaphoreType.DMA((copies,))] if copies else []),
        compiler_params=pltpu.CompilerParams(vmem_limit_bytes=28 << 20),
        cost_estimate=pl.CostEstimate(
            flops=products * 12 * 256 * 256 * 1024, bytes_accessed=4 << 20, transcendentals=1 << 18
        ),
    )

    def pinned(*values):
        return run(
            *[pltpu.with_memory_space_constraint(v, pltpu.HBM) if spec is HB else v for v, spec in zip(values, ins)]
        )

    return pinned


def on_device(image_embeds, text_embeds):
    images, texts = image_embeds[0, 0], text_embeds[0, 0]
    count, width = images.shape
    square, row, whole = ((count, count), f32), ((1, count), f32), ((count, width), f32)
    parts, left = ((3, count, width), bf16), ((count, len(PAIRS) * count), bf16)
    devices = lax.axis_size("dp") * lax.axis_size("hst")
    earlier_texts = from_behind(texts, "dp", 1)
    (
        logits, image_parts, self_rows, positive, self_columns, image_store, text_store, row_product, column_term
    ) = call(
        self_kernel,
        3,
        [HB, HB],
        [
            (VM, *square), (VM, *parts), (VM, *row), (VM, (1, 1), f32), (VM, *row),
            (HB, *parts), (HB, *parts), (HB, *whole), (HB, *whole),
        ],
        [whole, whole, parts, left, left, whole, whole],
        4,
    )(images, texts)
    before_columns = from_behind(self_columns, "dp", 1)
    later_rows = from_behind(self_rows, "dp", -1)
    earlier_texts, images, before_columns, later_rows, image_parts = lax.optimization_barrier(
        (earlier_texts, images, before_columns, later_rows, image_parts)
    )
    later_images = from_behind(images, "dp", -1)
    messages, weights, rows = call(
        earlier_kernel,
        1,
        [VM] * 5,
        [(VM, (devices, 1, LANES), f32), (VM, *square), (VM, *row)],
        [],
        0,
    )(image_parts, earlier_texts, self_rows, before_columns, positive)
    messages = lax.all_to_all(messages, ("dp", "hst"), 0, 0, tiled=True)
    image_part, row_term, text_parts = call(
        middle_kernel,
        2,
        [VM] * 5 + [HB] * 3,
        [(VM, *whole), (VM, *whole), (VM, *parts)],
        [parts, parts, whole, left, left],
        3,
    )(weights, earlier_texts, rows, logits, self_rows, image_store, text_store, row_product)
    image_grads, text_grads = call(
        last_kernel,
        3,
        [VM] * 7 + [HB],
        [(HB, *whole), (HB, *whole)],
        [parts, left, left, whole, whole, whole],
        5,
    )(text_parts, later_images, logits, later_rows, self_columns, image_part, row_term, column_term)
    messages, text_grads = lax.optimization_barrier((messages, text_grads))
    (mean_loss,) = call(functools.partial(loss_kernel, rows=count * devices), 0, [VM], [(VM, (1, 1), f32)], [], 0)(messages)
    return mean_loss[0, 0], image_grads[None, None], text_grads[None, None]


def solution(mesh):
    return jax.shard_map(
        on_device,
        mesh=mesh,
        in_specs=(P("dp", "hst", None, None), P("dp", "hst", None, None)),
        out_specs=(P(), P("dp", "hst", None, None), P("dp", "hst", None, None)),
        check_vma=False,
    )
```

```python
import functools

import jax
import jax.numpy as jnp
from jax import lax
from jax.experimental import pallas as pl
from jax.experimental.pallas import tpu as pltpu
from jax.sharding import PartitionSpec as P

logit_scale = 0.03125
f32, bf16 = jnp.float32, jnp.bfloat16
LANES = 128


def from_behind(value, axis, steps):
    count = lax.axis_size(axis)
    pairs = [(source, (source + steps) % count) for source in range(count)]
    return lax.ppermute(value, axis, pairs)


def split(value):
    high = value.astype(bf16)
    rest = value - high.astype(f32)
    middle = rest.astype(bf16)
    low = (rest - middle.astype(f32)).astype(bf16)
    return high, middle, low


PAIRS = ((2, 0), (1, 1), (0, 2), (1, 0), (0, 1), (0, 0))


def rows_by_rows(left, right):
    return lax.dot_general(
        jnp.concatenate([left[one] for one, _ in PAIRS], axis=1),
        jnp.concatenate([right[other] for _, other in PAIRS], axis=1),
        (((1,), (1,)), ((), ())),
        preferred_element_type=f32,
    )


def left_parts(left):
    parts = split(left)
    return jnp.concatenate([parts[one] for one, _ in PAIRS], axis=1)


def rows_by_columns(left, right):
    return jnp.dot(left, jnp.concatenate([right[other] for _, other in PAIRS], axis=0), preferred_element_type=f32)


def store_parts(stacked, value):
    for place, part in enumerate(split(value)):
        stacked[place] = part


def logsum(logits, axis):
    largest = jnp.max(logits, axis=axis, keepdims=True)
    return largest + jnp.log(jnp.sum(jnp.exp(logits - largest), axis=axis, keepdims=True))


def paired_logsum(former, latter):
    largest = jnp.maximum(former, latter)
    return largest + jnp.log(jnp.exp(former - largest) + jnp.exp(latter - largest))


def diagonal_mask(count):
    shape = (count, count)
    return lax.broadcasted_iota(jnp.int32, shape, 0) == lax.broadcasted_iota(jnp.int32, shape, 1)


def as_row(column, diagonal):
    return jnp.sum(jnp.where(diagonal, column, 0.0), axis=0, keepdims=True)


def as_column(row, diagonal):
    return jnp.sum(jnp.where(diagonal, row, 0.0), axis=1, keepdims=True)


def total(values):
    return jnp.sum(jnp.sum(values, axis=1, keepdims=True), axis=0, keepdims=True)


def start(pairs, semaphores):
    copies = [pltpu.make_async_copy(source, target, semaphores.at[k]) for k, (source, target) in enumerate(pairs)]
    for copy in copies:
        copy.start()
    return copies


def columns_at(k, size):
    return pl.ds(pl.multiple_of(k * size, size), size)


def self_kernel(
    images, texts,
    image_parts, row_part, positive, column_part, logits, image_store, text_store, row_product, column_term,
    own, image_in, text_in, text_parts, left, down, row_out, column_out, semaphores,
):
    copies = start([(images, image_in), (texts, text_in)], semaphores)
    copies[0].wait()
    store_parts(image_parts, image_in[...])
    copies[1].wait()
    store_parts(text_parts, text_in[...])
    copies = start([(image_parts, image_store), (text_parts, text_store)], semaphores)
    block = logit_scale * rows_by_rows(image_parts, text_parts)
    count, width = text_in.shape
    diagonal = diagonal_mask(count)
    rows, columns = logsum(block, 1), logsum(block, 0)
    own[...] = block
    row_part[...] = as_row(rows, diagonal)
    column_part[...] = columns
    positive[...] = as_row(block, diagonal)
    left[...] = left_parts(0.5 * jnp.exp(block - rows))
    down[...] = left_parts((0.5 * jnp.exp(block - columns)).T)
    half = width // 2

    @pl.loop(0, 2)
    def _(k):
        part = columns_at(k, half)
        row_out[:, part] = rows_by_columns(left[...], text_parts.at[:, :, part])
        column_out[:, part] = rows_by_columns(down[...], image_parts.at[:, :, part])

    copies += start([(row_out, row_product), (column_out, column_term), (own, logits)], semaphores.at[2:5])
    for copy in copies:
        copy.wait()


def earlier_kernel(
    image_parts, earlier_texts, self_rows, before_columns, positive,
    messages, weights, rows_out,
):
    block = logit_scale * rows_by_rows(image_parts, split(earlier_texts[...]))
    diagonal = diagonal_mask(block.shape[0])
    rows = paired_logsum(self_rows[...], as_row(logsum(block, 1), diagonal))
    columns = paired_logsum(before_columns[...], logsum(block, 0))
    partial = jnp.sum(0.5 * (rows + columns) - positive[...], axis=1, keepdims=True)
    messages[...] = jnp.broadcast_to(partial, messages.shape)
    weights[...] = 0.5 * (jnp.exp(block - as_column(rows, diagonal)) + jnp.exp(block - columns))
    rows_out[...] = rows


def middle_kernel(
    weights, earlier_texts, rows, self_rows, logits, image_store, text_store, row_store,
    image_part, row_term, text_parts, own,
    earlier_parts, image_parts, row_product, left, down, semaphores,
):
    copies = start(
        [(logits, own), (image_store, image_parts), (row_store, row_product), (text_store, text_parts)], semaphores
    )
    count, width = image_part.shape
    diagonal = diagonal_mask(count)
    left[...] = left_parts(weights[...])
    store_parts(earlier_parts, earlier_texts[...])
    joint = as_column(rows[...], diagonal)
    scale = as_column(jnp.exp(self_rows[...] - rows[...]), diagonal)
    half = width // 2

    @pl.loop(0, 2)
    def _(k):
        part = columns_at(k, half)
        image_part[:, part] = rows_by_columns(left[...], earlier_parts.at[:, :, part])

    copies[0].wait()
    down[...] = left_parts((0.5 * jnp.exp(own[...] - joint) - jnp.where(diagonal, 1.0, 0.0)).T)
    copies[1].wait()

    @pl.loop(0, 2)
    def _(k):
        part = columns_at(k, half)
        row_term[:, part] = rows_by_columns(down[...], image_parts.at[:, :, part])

    copies[2].wait()
    copies[3].wait()
    whole = text_parts[0].astype(f32) + text_parts[1].astype(f32) + text_parts[2].astype(f32)
    image_part[...] += scale * row_product[...] - whole


def first_kernel(text_parts, first, column_store, later_parts, product, column_term, semaphores):
    (copy,) = start([(column_store, column_term)], semaphores)
    part = slice(0, first.shape[1])
    store_parts(later_parts.at[:, :, part], first[...])
    product[...] = rows_by_rows(text_parts.at[:, :, part], later_parts.at[:, :, part])
    copy.wait()


def last_kernel(
    text_parts, first_parts, second, product, logits, later_rows, self_columns, image_part, row_term, column_term,
    later_parts, image_grads, text_grads,
    left, own_left, image_out, text_out, semaphores,
):
    count, width = image_out.shape
    diagonal = diagonal_mask(count)
    part = slice(width - second.shape[1], width)
    store_parts(later_parts.at[:, :, part], second[...])
    block = logit_scale * (product[...] + rows_by_rows(text_parts.at[:, :, part], later_parts.at[:, :, part]))
    rows = paired_logsum(later_rows[...], logsum(block, 0))
    own_columns = as_column(self_columns[...], diagonal)
    columns = paired_logsum(own_columns, logsum(block, 1))
    left[...] = left_parts(0.5 * (jnp.exp(block - rows) + jnp.exp(block - columns)))
    own_left[...] = left_parts(0.5 * jnp.exp(logits[...] - as_row(columns, diagonal)))
    scale = jnp.exp(own_columns - columns)
    half = width // 2

    def copies(k):
        part = columns_at(k, half)
        return (
            pltpu.make_async_copy(image_out.at[:, part], image_grads.at[:, part], semaphores.at[2 * k]),
            pltpu.make_async_copy(text_out.at[:, part], text_grads.at[:, part], semaphores.at[2 * k + 1]),
        )

    @pl.loop(0, 2)
    def _(k):
        part = columns_at(k, half)
        of_image, of_text = copies(k)
        terms = rows_by_columns(own_left[...], text_parts.at[:, :, part])
        image_out[:, part] = logit_scale * (image_part[:, part] + terms)
        of_image.start()
        terms = rows_by_columns(left[...], later_parts.at[:, :, part])
        text_out[:, part] = logit_scale * (row_term[:, part] + scale * column_term[:, part] + terms)
        of_text.start()

    for k in range(2):
        for copy in copies(k):
            copy.wait()


def loss_kernel(messages, mean_loss, *, rows):
    mean_loss[...] = total(messages[:, 0, 0:1]) / rows


VM, PV, HB = (pl.BlockSpec(memory_space=place) for place in (pltpu.VMEM, pltpu.VMEM, pltpu.HBM))


def call(kernel, products, ins, outs, scratch, copies, aliases=None):
    def shape_of(place, shape, dtype):
        if place is HB:
            return pltpu.HBM(shape, dtype)
        if place is PV:
            return pltpu.VMEM(shape, dtype)
        return jax.ShapeDtypeStruct(shape, dtype)

    run = pl.pallas_call(
        kernel,
        out_shape=[shape_of(*out) for out in outs],
        in_specs=ins,
        input_output_aliases=aliases or {},
        out_specs=[out[0] for out in outs],
        scratch_shapes=[pltpu.VMEM(shape, dtype) for shape, dtype in scratch]
        + ([pltpu.SemaphoreType.DMA((copies,))] if copies else []),
        compiler_params=pltpu.CompilerParams(vmem_limit_bytes=28 << 20),
        cost_estimate=pl.CostEstimate(
            flops=products * 12 * 256 * 256 * 1024, bytes_accessed=4 << 20, transcendentals=1 << 18
        ),
    )

    def pinned(*values):
        return run(
            *[pltpu.with_memory_space_constraint(v, pltpu.HBM) if spec is HB else v for v, spec in zip(values, ins)]
        )

    return pinned


def on_device(image_embeds, text_embeds):
    images, texts = image_embeds[0, 0], text_embeds[0, 0]
    count, width = images.shape
    small = width // 4
    square, row, whole = ((count, count), f32), ((1, count), f32), ((count, width), f32)
    parts, left = ((3, count, width), bf16), ((count, len(PAIRS) * count), bf16)
    devices = lax.axis_size("dp") * lax.axis_size("hst")
    earlier_texts = from_behind(texts, "dp", 1)
    (
        image_parts, self_rows, positive, self_columns, logits, image_store, text_store, row_product, column_term
    ) = call(
        self_kernel,
        3,
        [HB, HB],
        [
            (VM, *parts), (VM, *row), (VM, *row), (VM, *row),
            (HB, *square), (HB, *parts), (HB, *parts), (HB, *whole), (HB, *whole),
        ],
        [square, whole, whole, parts, left, left, whole, whole],
        5,
    )(images, texts)
    before_columns = from_behind(self_columns, "dp", 1)
    later_rows = from_behind(self_rows, "dp", -1)
    first, second = images[:, : width - small], images[:, width - small :]
    earlier_texts, first, second, before_columns, later_rows, image_parts = lax.optimization_barrier(
        (earlier_texts, first, second, before_columns, later_rows, image_parts)
    )
    first = from_behind(first, "dp", -1)
    second = from_behind(second, "dp", -1)
    messages, weights, rows = call(
        earlier_kernel,
        1,
        [VM] * 5,
        [(PV, (devices, 1, LANES), f32), (VM, *square), (VM, *row)],
        [],
        0,
    )(image_parts, earlier_texts, self_rows, before_columns, positive)
    messages = lax.all_to_all(messages, ("dp", "hst"), 0, 0, tiled=True)
    image_part, row_term, text_parts, logits = call(
        middle_kernel,
        2,
        [VM] * 4 + [HB] * 4,
        [(VM, *whole), (VM, *whole), (VM, *parts), (VM, *square)],
        [parts, parts, whole, left, left],
        4,
    )(weights, earlier_texts, rows, self_rows, logits, image_store, text_store, row_product)
    later_parts, product, column_term = call(
        first_kernel, 1, [VM, VM, HB], [(VM, *parts), (VM, *square), (VM, *whole)], [], 1
    )(text_parts, first, column_term)
    _, image_grads, text_grads = call(
        last_kernel,
        3,
        [VM] * 10,
        [(VM, *parts), (HB, *whole), (HB, *whole)],
        [left, left, whole, whole],
        4,
        {1: 0},
    )(text_parts, later_parts, second, product, logits, later_rows, self_columns, image_part, row_term, column_term)
    messages, text_grads = lax.optimization_barrier((messages, text_grads))
    (mean_loss,) = call(functools.partial(loss_kernel, rows=count * devices), 0, [VM], [(VM, (1, 1), f32)], [], 0)(messages)
    return mean_loss[0, 0], image_grads[None, None], text_grads[None, None]


def solution(mesh):
    return jax.shard_map(
        on_device,
        mesh=mesh,
        in_specs=(P("dp", "hst", None, None), P("dp", "hst", None, None)),
        out_specs=(P(), P("dp", "hst", None, None), P("dp", "hst", None, None)),
        check_vma=False,
    )
```

```python
import functools

import jax
import jax.numpy as jnp
from jax import lax
from jax.experimental import pallas as pl
from jax.experimental.pallas import tpu as pltpu
from jax.sharding import PartitionSpec as P

logit_scale = 0.03125
f32, bf16 = jnp.float32, jnp.bfloat16
LANES = 128


def from_behind(value, axis, steps):
    count = lax.axis_size(axis)
    pairs = [(source, (source + steps) % count) for source in range(count)]
    return lax.ppermute(value, axis, pairs)


def split(value):
    high = value.astype(bf16)
    rest = value - high.astype(f32)
    middle = rest.astype(bf16)
    low = (rest - middle.astype(f32)).astype(bf16)
    return high, middle, low


PAIRS = ((2, 0), (1, 1), (0, 2), (1, 0), (0, 1), (0, 0))


def rows_by_rows(left, right):
    return lax.dot_general(
        jnp.concatenate([left[one] for one, _ in PAIRS], axis=1),
        jnp.concatenate([right[other] for _, other in PAIRS], axis=1),
        (((1,), (1,)), ((), ())),
        preferred_element_type=f32,
    )


def left_parts(left):
    parts = split(left)
    return jnp.concatenate([parts[one] for one, _ in PAIRS], axis=1)


def rows_by_columns(left, right):
    return jnp.dot(left, jnp.concatenate([right[other] for _, other in PAIRS], axis=0), preferred_element_type=f32)


def store_parts(stacked, value):
    for place, part in enumerate(split(value)):
        stacked[place] = part


def logsum(logits, axis):
    largest = jnp.max(logits, axis=axis, keepdims=True)
    return largest + jnp.log(jnp.sum(jnp.exp(logits - largest), axis=axis, keepdims=True))


def paired_logsum(former, latter):
    largest = jnp.maximum(former, latter)
    return largest + jnp.log(jnp.exp(former - largest) + jnp.exp(latter - largest))


def joint_logsum(logits, other, axis):
    largest = jnp.max(logits, axis=axis, keepdims=True)
    powers = jnp.exp(logits - largest)
    joint = paired_logsum(other, largest + jnp.log(jnp.sum(powers, axis=axis, keepdims=True)))
    return joint, powers * (0.5 * jnp.exp(largest - joint))


def diagonal_mask(count):
    shape = (count, count)
    return lax.broadcasted_iota(jnp.int32, shape, 0) == lax.broadcasted_iota(jnp.int32, shape, 1)


def as_row(column, diagonal):
    return jnp.sum(jnp.where(diagonal, column, 0.0), axis=0, keepdims=True)


def as_column(row, diagonal):
    return jnp.sum(jnp.where(diagonal, row, 0.0), axis=1, keepdims=True)


def total(values):
    return jnp.sum(jnp.sum(values, axis=1, keepdims=True), axis=0, keepdims=True)


def start(pairs, semaphores):
    copies = [pltpu.make_async_copy(source, target, semaphores.at[k]) for k, (source, target) in enumerate(pairs)]
    for copy in copies:
        copy.start()
    return copies


def columns_at(k, size):
    return pl.ds(pl.multiple_of(k * size, size), size)


def self_kernel(
    images, texts,
    image_parts, row_part, columns_out, first, second, logits, image_store, text_store, row_product, column_term,
    own, image_in, text_in, text_parts, left, down, row_out, column_out, semaphores,
):
    copies = start([(images, image_in), (texts, text_in)], semaphores)
    copies[0].wait()
    store_parts(image_parts, image_in[...])
    border = first.shape[1]
    first[...] = image_in[:, :border]
    sent = start([(image_in.at[:, border:], second)], semaphores.at[5:6])
    copies[1].wait()
    store_parts(text_parts, text_in[...])
    copies = start([(image_parts, image_store), (text_parts, text_store)], semaphores)
    block = logit_scale * rows_by_rows(image_parts, text_parts)
    count, width = text_in.shape
    diagonal = diagonal_mask(count)
    rows, columns = logsum(block, 1), logsum(block, 0)
    own[...] = block
    row_part[...] = as_row(rows, diagonal)
    columns_out[0:1, :] = columns
    columns_out[1:2, :] = as_row(block, diagonal)
    left[...] = left_parts(jnp.where(diagonal, 0.0, 0.5 * jnp.exp(block - rows)))
    down[...] = left_parts(jnp.where(diagonal, 0.0, 0.5 * jnp.exp(block - columns)).T)
    half = width // 2

    @pl.loop(0, 2)
    def _(k):
        part = columns_at(k, half)
        row_out[:, part] = rows_by_columns(left[...], text_parts.at[:, :, part])
        column_out[:, part] = rows_by_columns(down[...], image_parts.at[:, :, part])

    copies += start([(row_out, row_product), (column_out, column_term), (own, logits)], semaphores.at[2:5])
    copies += sent
    for copy in copies:
        copy.wait()


def earlier_kernel(
    image_parts, earlier_texts, self_rows, self_columns, before_columns,
    messages, weights, rows_out,
):
    block = logit_scale * rows_by_rows(image_parts, split(earlier_texts[...]))
    diagonal = diagonal_mask(block.shape[0])
    rows = paired_logsum(self_rows[...], as_row(logsum(block, 1), diagonal))
    columns = paired_logsum(before_columns[0:1, :], logsum(block, 0))
    partial = 0.5 * jnp.sum((rows - self_columns[1:2, :]) + (columns - before_columns[1:2, :]), axis=1, keepdims=True)
    messages[...] = jnp.broadcast_to(partial, messages.shape)
    weights[...] = 0.5 * (jnp.exp(block - as_column(rows, diagonal)) + jnp.exp(block - columns))
    rows_out[...] = rows


def middle_kernel(
    weights, earlier_texts, rows, self_rows, logits, image_store, text_store, row_store,
    image_part, row_term, text_parts, own,
    earlier_parts, image_parts, row_product, left, down, semaphores,
):
    copies = start(
        [(logits, own), (image_store, image_parts), (row_store, row_product), (text_store, text_parts)], semaphores
    )
    count, width = image_part.shape
    diagonal = diagonal_mask(count)
    left[...] = left_parts(weights[...])
    store_parts(earlier_parts, earlier_texts[...])
    joint = as_column(rows[...], diagonal)
    scale = as_column(jnp.exp(self_rows[...] - rows[...]), diagonal)
    half = width // 2

    @pl.loop(0, 2)
    def _(k):
        part = columns_at(k, half)
        image_part[:, part] = rows_by_columns(left[...], earlier_parts.at[:, :, part])

    copies[0].wait()
    down[...] = left_parts(jnp.where(diagonal, 0.0, 0.5 * jnp.exp(own[...] - joint)).T)
    copies[1].wait()

    @pl.loop(0, 2)
    def _(k):
        part = columns_at(k, half)
        row_term[:, part] = rows_by_columns(down[...], image_parts.at[:, :, part])

    copies[2].wait()
    image_part[...] += scale * row_product[...]
    copies[3].wait()


def first_kernel(text_parts, first, column_store, images, later_parts, product, column_term, own_images, semaphores):
    copies = start([(column_store, column_term), (images, own_images)], semaphores)
    part = slice(0, first.shape[1])
    store_parts(later_parts.at[:, :, part], first[...])
    product[...] = rows_by_rows(text_parts.at[:, :, part], later_parts.at[:, :, part])
    for copy in copies:
        copy.wait()


def last_kernel(
    text_parts, first_parts, second, product, logits, rows_in, later_rows, self_columns, image_part, row_term, column_term, image_in,
    later_parts, image_grads, text_grads,
    left, own_left, image_out, text_out, semaphores,
):
    count, width = image_out.shape
    diagonal = diagonal_mask(count)
    part = slice(width - second.shape[1], width)
    store_parts(later_parts.at[:, :, part], second[...])
    block = logit_scale * (product[...] + rows_by_rows(text_parts.at[:, :, part], later_parts.at[:, :, part]))
    own_columns = as_column(self_columns[0:1, :], diagonal)
    rows, by_rows = joint_logsum(block, later_rows[...], 0)
    columns, by_columns = joint_logsum(block, own_columns, 1)
    left[...] = left_parts(by_rows + by_columns)
    across, positive = as_row(columns, diagonal), self_columns[1:2, :]
    own = 0.5 * (jnp.exp(positive - rows_in[...]) + jnp.exp(positive - across)) - 1.0
    own_left[...] = left_parts(jnp.where(diagonal, own, 0.5 * jnp.exp(logits[...] - across)))
    own_down = as_column(own, diagonal)
    scale = jnp.exp(own_columns - columns)
    half = width // 2

    def copies(k):
        part = columns_at(k, half)
        return (
            pltpu.make_async_copy(image_out.at[:, part], image_grads.at[:, part], semaphores.at[2 * k]),
            pltpu.make_async_copy(text_out.at[:, part], text_grads.at[:, part], semaphores.at[2 * k + 1]),
        )

    @pl.loop(0, 2)
    def _(k):
        part = columns_at(k, half)
        of_image, of_text = copies(k)
        terms = rows_by_columns(own_left[...], text_parts.at[:, :, part])
        image_out[:, part] = logit_scale * (image_part[:, part] + terms)
        of_image.start()
        terms = rows_by_columns(left[...], later_parts.at[:, :, part])
        own_terms = row_term[:, part] + scale * column_term[:, part] + own_down * image_in[:, part]
        text_out[:, part] = logit_scale * (own_terms + terms)
        of_text.start()

    for k in range(2):
        for copy in copies(k):
            copy.wait()


def loss_kernel(messages, mean_loss, *, rows):
    mean_loss[...] = total(messages[:, 0, 0:1]) / rows


VM, PV, HB = (pl.BlockSpec(memory_space=place) for place in (pltpu.VMEM, pltpu.VMEM, pltpu.HBM))


def call(kernel, products, ins, outs, scratch, copies, aliases=None):
    def shape_of(place, shape, dtype):
        if place is HB:
            return pltpu.HBM(shape, dtype)
        if place is PV:
            return pltpu.VMEM(shape, dtype)
        return jax.ShapeDtypeStruct(shape, dtype)

    run = pl.pallas_call(
        kernel,
        out_shape=[shape_of(*out) for out in outs],
        in_specs=ins,
        input_output_aliases=aliases or {},
        out_specs=[out[0] for out in outs],
        scratch_shapes=[pltpu.VMEM(shape, dtype) for shape, dtype in scratch]
        + ([pltpu.SemaphoreType.DMA((copies,))] if copies else []),
        compiler_params=pltpu.CompilerParams(vmem_limit_bytes=28 << 20),
        cost_estimate=pl.CostEstimate(
            flops=products * 12 * 256 * 256 * 1024, bytes_accessed=4 << 20, transcendentals=1 << 18
        ),
    )

    def pinned(*values):
        return run(
            *[pltpu.with_memory_space_constraint(v, pltpu.HBM) if spec is HB else v for v, spec in zip(values, ins)]
        )

    return pinned


def on_device(image_embeds, text_embeds):
    images, texts = image_embeds[0, 0], text_embeds[0, 0]
    count, width = images.shape
    small = width // 4
    square, row, whole = ((count, count), f32), ((1, count), f32), ((count, width), f32)
    parts, left = ((3, count, width), bf16), ((count, len(PAIRS) * count), bf16)
    devices = lax.axis_size("dp") * lax.axis_size("hst")
    earlier_texts = from_behind(texts, "dp", 1)
    (
        image_parts, self_rows, self_columns, first, second, logits, image_store, text_store, row_product, column_term
    ) = call(
        self_kernel,
        3,
        [HB, HB],
        [
            (VM, *parts), (VM, *row), (VM, (2, count), f32),
            (PV, (count, width - small), f32), (HB, (count, small), f32), (HB, *square), (HB, *parts), (HB, *parts), (HB, *whole), (HB, *whole),
        ],
        [square, whole, whole, parts, left, left, whole, whole],
        6,
    )(images, texts)
    before_columns = from_behind(self_columns, "dp", 1)
    later_rows = from_behind(self_rows, "dp", -1)
    earlier_texts, first, second, before_columns, later_rows, image_parts = lax.optimization_barrier(
        (earlier_texts, first, second, before_columns, later_rows, image_parts)
    )
    first = from_behind(first, "dp", -1)
    second = from_behind(second, "dp", -1)
    messages, weights, rows = call(
        earlier_kernel,
        1,
        [VM] * 5,
        [(PV, (devices, 1, LANES), f32), (VM, *square), (VM, *row)],
        [],
        0,
    )(image_parts, earlier_texts, self_rows, self_columns, before_columns)
    messages = lax.all_to_all(messages, ("dp", "hst"), 0, 0, tiled=True)
    image_part, row_term, text_parts, logits = call(
        middle_kernel,
        2,
        [VM] * 4 + [HB] * 4,
        [(VM, *whole), (VM, *whole), (VM, *parts), (VM, *square)],
        [parts, parts, whole, left, left],
        4,
    )(weights, earlier_texts, rows, self_rows, logits, image_store, text_store, row_product)
    later_parts, product, column_term, images = call(
        first_kernel, 1, [VM, VM, HB, HB], [(VM, *parts), (VM, *square), (VM, *whole), (VM, *whole)], [], 2
    )(text_parts, first, column_term, images)
    _, image_grads, text_grads = call(
        last_kernel,
        3,
        [VM] * 12,
        [(VM, *parts), (HB, *whole), (HB, *whole)],
        [left, left, whole, whole],
        4,
        {1: 0},
    )(
        text_parts, later_parts, second, product, logits, rows, later_rows, self_columns, image_part, row_term, column_term, images
    )
    messages, text_grads = lax.optimization_barrier((messages, text_grads))
    (mean_loss,) = call(functools.partial(loss_kernel, rows=count * devices), 0, [VM], [(VM, (1, 1), f32)], [], 0)(messages)
    return mean_loss[0, 0], image_grads[None, None], text_grads[None, None]


def solution(mesh):
    return jax.shard_map(
        on_device,
        mesh=mesh,
        in_specs=(P("dp", "hst", None, None), P("dp", "hst", None, None)),
        out_specs=(P(), P("dp", "hst", None, None), P("dp", "hst", None, None)),
        check_vma=False,
    )
```

```python
import functools

import jax
import jax.numpy as jnp
from jax import lax
from jax.experimental import pallas as pl
from jax.experimental.pallas import tpu as pltpu
from jax.sharding import PartitionSpec as P

logit_scale = 0.03125
f32, bf16 = jnp.float32, jnp.bfloat16
LANES = 128


def from_behind(value, axis, steps):
    count = lax.axis_size(axis)
    pairs = [(source, (source + steps) % count) for source in range(count)]
    return lax.ppermute(value, axis, pairs)


def split(value):
    high = value.astype(bf16)
    rest = value - high.astype(f32)
    middle = rest.astype(bf16)
    low = (rest - middle.astype(f32)).astype(bf16)
    return high, middle, low


PAIRS = ((2, 0), (1, 1), (0, 2), (1, 0), (0, 1), (0, 0))


def rows_by_rows(left, right):
    return lax.dot_general(
        jnp.concatenate([left[one] for one, _ in PAIRS], axis=1),
        jnp.concatenate([right[other] for _, other in PAIRS], axis=1),
        (((1,), (1,)), ((), ())),
        preferred_element_type=f32,
    )


def left_parts(left):
    parts = split(left)
    return jnp.concatenate([parts[one] for one, _ in PAIRS], axis=1)


def rows_by_columns(left, right):
    return jnp.dot(left, jnp.concatenate([right[other] for _, other in PAIRS], axis=0), preferred_element_type=f32)


def store_parts(stacked, value):
    for place, part in enumerate(split(value)):
        stacked[place] = part


def logsum(logits, axis):
    largest = jnp.max(logits, axis=axis, keepdims=True)
    return largest + jnp.log(jnp.sum(jnp.exp(logits - largest), axis=axis, keepdims=True))


def paired_logsum(former, latter):
    largest = jnp.maximum(former, latter)
    return largest + jnp.log(jnp.exp(former - largest) + jnp.exp(latter - largest))


def joint_logsum(logits, other, axis):
    largest = jnp.max(logits, axis=axis, keepdims=True)
    powers = jnp.exp(logits - largest)
    joint = paired_logsum(other, largest + jnp.log(jnp.sum(powers, axis=axis, keepdims=True)))
    return joint, powers * (0.5 * jnp.exp(largest - joint))


def diagonal_mask(count):
    shape = (count, count)
    return lax.broadcasted_iota(jnp.int32, shape, 0) == lax.broadcasted_iota(jnp.int32, shape, 1)


def as_row(column, diagonal):
    return jnp.sum(jnp.where(diagonal, column, 0.0), axis=0, keepdims=True)


def as_column(row, diagonal):
    return jnp.sum(jnp.where(diagonal, row, 0.0), axis=1, keepdims=True)


def total(values):
    return jnp.sum(jnp.sum(values, axis=1, keepdims=True), axis=0, keepdims=True)


def start(pairs, semaphores):
    copies = [pltpu.make_async_copy(source, target, semaphores.at[k]) for k, (source, target) in enumerate(pairs)]
    for copy in copies:
        copy.start()
    return copies


def columns_at(k, size):
    return pl.ds(pl.multiple_of(k * size, size), size)


def self_kernel(
    images, texts,
    image_parts, row_part, columns_out, first, second, logits, image_store, text_store, row_product, column_term,
    own, image_in, text_in, text_parts, left, down, row_out, column_out, semaphores,
):
    copies = start([(images, image_in), (texts, text_in)], semaphores)
    copies[0].wait()
    store_parts(image_parts, image_in[...])
    border = first.shape[1]
    first[...] = image_in[:, :border]
    second[...] = image_in[:, border:]
    copies[1].wait()
    store_parts(text_parts, text_in[...])
    copies = start([(image_parts, image_store), (text_parts, text_store)], semaphores)
    block = logit_scale * rows_by_rows(image_parts, text_parts)
    count, width = text_in.shape
    diagonal = diagonal_mask(count)
    rows, columns = logsum(block, 1), logsum(block, 0)
    own[...] = block
    row_part[...] = as_row(rows, diagonal)
    columns_out[0:1, :] = columns
    columns_out[1:2, :] = as_row(block, diagonal)
    left[...] = left_parts(jnp.where(diagonal, 0.0, 0.5 * jnp.exp(block - rows)))
    down[...] = left_parts(jnp.where(diagonal, 0.0, 0.5 * jnp.exp(block - columns)).T)
    half = width // 2

    @pl.loop(0, 2)
    def _(k):
        part = columns_at(k, half)
        row_out[:, part] = rows_by_columns(left[...], text_parts.at[:, :, part])
        column_out[:, part] = rows_by_columns(down[...], image_parts.at[:, :, part])

    copies += start([(row_out, row_product), (column_out, column_term), (own, logits)], semaphores.at[2:5])
    for copy in copies:
        copy.wait()


def earlier_kernel(
    image_parts, earlier_texts, self_rows, self_columns, before_columns,
    messages, weights, rows_out,
    letters, semaphores,
):
    block = logit_scale * rows_by_rows(image_parts, split(earlier_texts[...]))
    diagonal = diagonal_mask(block.shape[0])
    rows = paired_logsum(self_rows[...], as_row(logsum(block, 1), diagonal))
    columns = paired_logsum(before_columns[0:1, :], logsum(block, 0))
    partial = 0.5 * jnp.sum((rows - self_columns[1:2, :]) + (columns - before_columns[1:2, :]), axis=1, keepdims=True)
    letters[...] = jnp.broadcast_to(partial, letters.shape)
    (copy,) = start([(letters, messages)], semaphores)
    weights[...] = 0.5 * (jnp.exp(block - as_column(rows, diagonal)) + jnp.exp(block - columns))
    rows_out[...] = rows
    copy.wait()


def middle_kernel(
    weights, earlier_texts, rows, self_rows, logits, image_store, text_store, row_store,
    image_part, row_term, text_parts, own,
    earlier_parts, image_parts, row_product, left, down, semaphores,
):
    copies = start(
        [(logits, own), (image_store, image_parts), (row_store, row_product), (text_store, text_parts)], semaphores
    )
    count, width = image_part.shape
    diagonal = diagonal_mask(count)
    left[...] = left_parts(weights[...])
    store_parts(earlier_parts, earlier_texts[...])
    joint = as_column(rows[...], diagonal)
    scale = as_column(jnp.exp(self_rows[...] - rows[...]), diagonal)
    half = width // 2

    @pl.loop(0, 2)
    def _(k):
        part = columns_at(k, half)
        image_part[:, part] = rows_by_columns(left[...], earlier_parts.at[:, :, part])

    copies[0].wait()
    down[...] = left_parts(jnp.where(diagonal, 0.0, 0.5 * jnp.exp(own[...] - joint)).T)
    copies[1].wait()

    @pl.loop(0, 2)
    def _(k):
        part = columns_at(k, half)
        row_term[:, part] = rows_by_columns(down[...], image_parts.at[:, :, part])

    copies[2].wait()
    image_part[...] += scale * row_product[...]
    copies[3].wait()


def first_kernel(text_parts, first, column_store, images, later_parts, product, column_term, own_images, semaphores):
    copies = start([(column_store, column_term), (images, own_images)], semaphores)
    part = slice(0, first.shape[1])
    store_parts(later_parts.at[:, :, part], first[...])
    product[...] = rows_by_rows(text_parts.at[:, :, part], later_parts.at[:, :, part])
    for copy in copies:
        copy.wait()


def last_kernel(
    text_parts, first_parts, second, product, logits, rows_in, later_rows, self_columns, image_part, row_term, column_term, image_in,
    later_parts, image_grads, text_grads,
    left, own_left, image_out, text_out, semaphores,
):
    count, width = image_out.shape
    diagonal = diagonal_mask(count)
    part = slice(width - second.shape[1], width)
    store_parts(later_parts.at[:, :, part], second[...])
    block = logit_scale * (product[...] + rows_by_rows(text_parts.at[:, :, part], later_parts.at[:, :, part]))
    own_columns = as_column(self_columns[0:1, :], diagonal)
    rows, by_rows = joint_logsum(block, later_rows[...], 0)
    columns, by_columns = joint_logsum(block, own_columns, 1)
    left[...] = left_parts(by_rows + by_columns)
    across, positive = as_row(columns, diagonal), self_columns[1:2, :]
    own = 0.5 * (jnp.exp(positive - rows_in[...]) + jnp.exp(positive - across)) - 1.0
    own_left[...] = left_parts(jnp.where(diagonal, own, 0.5 * jnp.exp(logits[...] - across)))
    own_down = as_column(own, diagonal)
    scale = jnp.exp(own_columns - columns)
    half = width // 2

    def copies(k):
        part = columns_at(k, half)
        return (
            pltpu.make_async_copy(image_out.at[:, part], image_grads.at[:, part], semaphores.at[2 * k]),
            pltpu.make_async_copy(text_out.at[:, part], text_grads.at[:, part], semaphores.at[2 * k + 1]),
        )

    @pl.loop(0, 2)
    def _(k):
        part = columns_at(k, half)
        of_image, of_text = copies(k)
        terms = rows_by_columns(own_left[...], text_parts.at[:, :, part])
        image_out[:, part] = logit_scale * (image_part[:, part] + terms)
        of_image.start()
        terms = rows_by_columns(left[...], later_parts.at[:, :, part])
        own_terms = row_term[:, part] + scale * column_term[:, part] + own_down * image_in[:, part]
        text_out[:, part] = logit_scale * (own_terms + terms)
        of_text.start()

    for k in range(2):
        for copy in copies(k):
            copy.wait()


def loss_kernel(messages, mean_loss, *, rows):
    mean_loss[...] = total(messages[:, 0, 0:1]) / rows


VM, PV, HB = (pl.BlockSpec(memory_space=place) for place in (pltpu.VMEM, pltpu.VMEM, pltpu.HBM))


def call(kernel, products, ins, outs, scratch, copies, aliases=None):
    def shape_of(place, shape, dtype):
        if place is HB:
            return pltpu.HBM(shape, dtype)
        if place is PV:
            return pltpu.VMEM(shape, dtype)
        return jax.ShapeDtypeStruct(shape, dtype)

    run = pl.pallas_call(
        kernel,
        out_shape=[shape_of(*out) for out in outs],
        in_specs=ins,
        input_output_aliases=aliases or {},
        out_specs=[out[0] for out in outs],
        scratch_shapes=[pltpu.VMEM(shape, dtype) for shape, dtype in scratch]
        + ([pltpu.SemaphoreType.DMA((copies,))] if copies else []),
        compiler_params=pltpu.CompilerParams(vmem_limit_bytes=28 << 20),
        cost_estimate=pl.CostEstimate(
            flops=products * 12 * 256 * 256 * 1024, bytes_accessed=4 << 20, transcendentals=1 << 18
        ),
    )

    def pinned(*values):
        return run(
            *[pltpu.with_memory_space_constraint(v, pltpu.HBM) if spec is HB else v for v, spec in zip(values, ins)]
        )

    return pinned


def on_device(image_embeds, text_embeds):
    images, texts = image_embeds[0, 0], text_embeds[0, 0]
    count, width = images.shape
    small = width // 4
    square, row, whole = ((count, count), f32), ((1, count), f32), ((count, width), f32)
    parts, left = ((3, count, width), bf16), ((count, len(PAIRS) * count), bf16)
    devices = lax.axis_size("dp") * lax.axis_size("hst")
    earlier_texts = from_behind(texts, "dp", 1)
    (
        image_parts, self_rows, self_columns, first, second, logits, image_store, text_store, row_product, column_term
    ) = call(
        self_kernel,
        3,
        [HB, HB],
        [
            (VM, *parts), (VM, *row), (VM, (2, count), f32),
            (PV, (count, width - small), f32), (PV, (count, small), f32), (HB, *square), (HB, *parts), (HB, *parts), (HB, *whole), (HB, *whole),
        ],
        [square, whole, whole, parts, left, left, whole, whole],
        6,
    )(images, texts)
    before_columns = from_behind(self_columns, "dp", 1)
    later_rows = from_behind(self_rows, "dp", -1)
    earlier_texts, first, second, before_columns, later_rows, image_parts = lax.optimization_barrier(
        (earlier_texts, first, second, before_columns, later_rows, image_parts)
    )
    first = from_behind(first, "dp", -1)
    messages, weights, rows = call(
        earlier_kernel,
        1,
        [VM] * 5,
        [(HB, (devices, 1, LANES), f32), (VM, *square), (VM, *row)],
        [((devices, 1, LANES), f32)],
        1,
    )(image_parts, earlier_texts, self_rows, self_columns, before_columns)
    second, weights = lax.optimization_barrier((second, weights))
    second = from_behind(second, "dp", -1)
    messages = lax.all_to_all(messages, ("dp", "hst"), 0, 0, tiled=True)
    image_part, row_term, text_parts, logits = call(
        middle_kernel,
        2,
        [VM] * 4 + [HB] * 4,
        [(VM, *whole), (VM, *whole), (VM, *parts), (VM, *square)],
        [parts, parts, whole, left, left],
        4,
    )(weights, earlier_texts, rows, self_rows, logits, image_store, text_store, row_product)
    later_parts, product, column_term, images = call(
        first_kernel, 1, [VM, VM, HB, HB], [(VM, *parts), (VM, *square), (VM, *whole), (VM, *whole)], [], 2
    )(text_parts, first, column_term, images)
    _, image_grads, text_grads = call(
        last_kernel,
        3,
        [VM] * 12,
        [(VM, *parts), (HB, *whole), (HB, *whole)],
        [left, left, whole, whole],
        4,
        {1: 0},
    )(
        text_parts, later_parts, second, product, logits, rows, later_rows, self_columns, image_part, row_term, column_term, images
    )
    messages, text_grads = lax.optimization_barrier((messages, text_grads))
    (mean_loss,) = call(functools.partial(loss_kernel, rows=count * devices), 0, [VM], [(VM, (1, 1), f32)], [], 0)(messages)
    return mean_loss[0, 0], image_grads[None, None], text_grads[None, None]


def solution(mesh):
    return jax.shard_map(
        on_device,
        mesh=mesh,
        in_specs=(P("dp", "hst", None, None), P("dp", "hst", None, None)),
        out_specs=(P(), P("dp", "hst", None, None), P("dp", "hst", None, None)),
        check_vma=False,
    )
```

```python
import functools

import jax
import jax.numpy as jnp
from jax import lax
from jax.experimental import pallas as pl
from jax.experimental.pallas import tpu as pltpu
from jax.sharding import PartitionSpec as P

logit_scale = 0.03125
f32, bf16 = jnp.float32, jnp.bfloat16
LANES = 128


def from_behind(value, axis, steps):
    count = lax.axis_size(axis)
    pairs = [(source, (source + steps) % count) for source in range(count)]
    return lax.ppermute(value, axis, pairs)


def split(value):
    high = value.astype(bf16)
    rest = value - high.astype(f32)
    middle = rest.astype(bf16)
    low = (rest - middle.astype(f32)).astype(bf16)
    return high, middle, low


PAIRS = ((2, 0), (1, 1), (0, 2), (1, 0), (0, 1), (0, 0))


def rows_by_rows(left, right):
    return lax.dot_general(
        jnp.concatenate([left[one] for one, _ in PAIRS], axis=1),
        jnp.concatenate([right[other] for _, other in PAIRS], axis=1),
        (((1,), (1,)), ((), ())),
        preferred_element_type=f32,
    )


def left_parts(left):
    parts = split(left)
    return jnp.concatenate([parts[one] for one, _ in PAIRS], axis=1)


def rows_by_columns(left, right):
    return jnp.dot(left, jnp.concatenate([right[other] for _, other in PAIRS], axis=0), preferred_element_type=f32)


def store_parts(stacked, value):
    for place, part in enumerate(split(value)):
        stacked[place] = part


def logsum(logits, axis):
    largest = jnp.max(logits, axis=axis, keepdims=True)
    return largest + jnp.log(jnp.sum(jnp.exp(logits - largest), axis=axis, keepdims=True))


def paired_logsum(former, latter):
    largest = jnp.maximum(former, latter)
    return largest + jnp.log(jnp.exp(former - largest) + jnp.exp(latter - largest))


def joint_logsum(logits, other, axis):
    largest = jnp.max(logits, axis=axis, keepdims=True)
    powers = jnp.exp(logits - largest)
    joint = paired_logsum(other, largest + jnp.log(jnp.sum(powers, axis=axis, keepdims=True)))
    return joint, powers * (0.5 * jnp.exp(largest - joint))


def diagonal_mask(count):
    shape = (count, count)
    return lax.broadcasted_iota(jnp.int32, shape, 0) == lax.broadcasted_iota(jnp.int32, shape, 1)


def as_row(column, diagonal):
    return jnp.sum(jnp.where(diagonal, column, 0.0), axis=0, keepdims=True)


def as_column(row, diagonal):
    return jnp.sum(jnp.where(diagonal, row, 0.0), axis=1, keepdims=True)


def total(values):
    return jnp.sum(jnp.sum(values, axis=1, keepdims=True), axis=0, keepdims=True)


def start(pairs, semaphores):
    copies = [pltpu.make_async_copy(source, target, semaphores.at[k]) for k, (source, target) in enumerate(pairs)]
    for copy in copies:
        copy.start()
    return copies


def columns_at(k, size):
    return pl.ds(pl.multiple_of(k * size, size), size)


def self_kernel(
    images, texts,
    image_parts, row_part, columns_out, first, second, logits, image_store, text_store, row_product, column_term,
    own, image_in, text_in, text_parts, left, down, row_out, column_out, semaphores,
):
    copies = start([(images, image_in), (texts, text_in)], semaphores)
    copies[0].wait()
    store_parts(image_parts, image_in[...])
    border = first.shape[1]
    first[...] = image_in[:, :border]
    second[...] = image_in[:, border:]
    copies[1].wait()
    store_parts(text_parts, text_in[...])
    copies = start([(image_parts, image_store), (text_parts, text_store)], semaphores)
    block = logit_scale * rows_by_rows(image_parts, text_parts)
    count, width = text_in.shape
    diagonal = diagonal_mask(count)
    rows, columns = logsum(block, 1), logsum(block, 0)
    own[...] = block
    row_part[...] = as_row(rows, diagonal)
    columns_out[0:1, :] = columns
    columns_out[1:2, :] = as_row(block, diagonal)
    left[...] = left_parts(jnp.where(diagonal, 0.0, 0.5 * jnp.exp(block - rows)))
    down[...] = left_parts(jnp.where(diagonal, 0.0, 0.5 * jnp.exp(block - columns)).T)
    half = width // 2

    @pl.loop(0, 2)
    def _(k):
        part = columns_at(k, half)
        row_out[:, part] = rows_by_columns(left[...], text_parts.at[:, :, part])
        column_out[:, part] = rows_by_columns(down[...], image_parts.at[:, :, part])

    copies += start([(row_out, row_product), (column_out, column_term), (own, logits)], semaphores.at[2:5])
    for copy in copies:
        copy.wait()


def earlier_kernel(
    image_parts, earlier_texts, self_rows, self_columns, before_columns,
    messages, weights, rows_out,
    letters, semaphores,
):
    block = logit_scale * rows_by_rows(image_parts, split(earlier_texts[...]))
    diagonal = diagonal_mask(block.shape[0])
    rows = paired_logsum(self_rows[...], as_row(logsum(block, 1), diagonal))
    columns = paired_logsum(before_columns[0:1, :], logsum(block, 0))
    partial = 0.5 * jnp.sum((rows - self_columns[1:2, :]) + (columns - before_columns[1:2, :]), axis=1, keepdims=True)
    letters[...] = jnp.broadcast_to(partial, letters.shape)
    (copy,) = start([(letters, messages)], semaphores)
    weights[...] = 0.5 * (jnp.exp(block - as_column(rows, diagonal)) + jnp.exp(block - columns))
    rows_out[...] = rows
    copy.wait()


def middle_kernel(
    weights, earlier_texts, rows, self_rows, logits, image_store, text_store, row_store,
    image_part, row_term, text_parts, own,
    earlier_parts, image_parts, row_product, left, down, semaphores,
):
    copies = start(
        [(logits, own), (image_store, image_parts), (row_store, row_product), (text_store, text_parts)], semaphores
    )
    count, width = image_part.shape
    diagonal = diagonal_mask(count)
    left[...] = left_parts(weights[...])
    store_parts(earlier_parts, earlier_texts[...])
    joint = as_column(rows[...], diagonal)
    scale = as_column(jnp.exp(self_rows[...] - rows[...]), diagonal)
    half = width // 2

    @pl.loop(0, 2)
    def _(k):
        part = columns_at(k, half)
        image_part[:, part] = rows_by_columns(left[...], earlier_parts.at[:, :, part])

    copies[0].wait()
    down[...] = left_parts(jnp.where(diagonal, 0.0, 0.5 * jnp.exp(own[...] - joint)).T)
    copies[1].wait()

    @pl.loop(0, 2)
    def _(k):
        part = columns_at(k, half)
        row_term[:, part] = rows_by_columns(down[...], image_parts.at[:, :, part])

    copies[2].wait()
    image_part[...] += scale * row_product[...]
    copies[3].wait()


def first_kernel(text_parts, first, column_store, images, first_parts, product, column_term, own_images, semaphores):
    copies = start([(column_store, column_term), (images, own_images)], semaphores)
    store_parts(first_parts, first[...])
    product[...] = rows_by_rows(text_parts.at[:, :, : first.shape[1]], first_parts)
    for copy in copies:
        copy.wait()


def last_kernel(
    text_parts, first_parts, second, product, logits, rows_in, later_rows, self_columns, image_part, row_term, column_term, image_in,
    image_grads, text_grads,
    later_parts, left, own_left, image_out, text_out, semaphores,
):
    count, width = image_out.shape
    diagonal = diagonal_mask(count)
    border = first_parts.shape[2]
    part = slice(border, width)
    later_parts[:, :, :border] = first_parts[...]
    store_parts(later_parts.at[:, :, part], second[...])
    block = logit_scale * (product[...] + rows_by_rows(text_parts.at[:, :, part], later_parts.at[:, :, part]))
    own_columns = as_column(self_columns[0:1, :], diagonal)
    rows, by_rows = joint_logsum(block, later_rows[...], 0)
    columns, by_columns = joint_logsum(block, own_columns, 1)
    left[...] = left_parts(by_rows + by_columns)
    across, positive = as_row(columns, diagonal), self_columns[1:2, :]
    own = 0.5 * (jnp.exp(positive - rows_in[...]) + jnp.exp(positive - across)) - 1.0
    own_left[...] = left_parts(jnp.where(diagonal, own, 0.5 * jnp.exp(logits[...] - across)))
    own_down = as_column(own, diagonal)
    scale = jnp.exp(own_columns - columns)
    half = width // 2

    def copies(k):
        part = columns_at(k, half)
        return (
            pltpu.make_async_copy(image_out.at[:, part], image_grads.at[:, part], semaphores.at[2 * k]),
            pltpu.make_async_copy(text_out.at[:, part], text_grads.at[:, part], semaphores.at[2 * k + 1]),
        )

    @pl.loop(0, 2)
    def _(k):
        part = columns_at(k, half)
        of_image, of_text = copies(k)
        terms = rows_by_columns(own_left[...], text_parts.at[:, :, part])
        image_out[:, part] = logit_scale * (image_part[:, part] + terms)
        of_image.start()
        terms = rows_by_columns(left[...], later_parts.at[:, :, part])
        own_terms = row_term[:, part] + scale * column_term[:, part] + own_down * image_in[:, part]
        text_out[:, part] = logit_scale * (own_terms + terms)
        of_text.start()

    for k in range(2):
        for copy in copies(k):
            copy.wait()


def loss_kernel(messages, mean_loss, *, rows):
    mean_loss[...] = total(messages[:, 0, 0:1]) / rows


VM, PV, HB = (pl.BlockSpec(memory_space=place) for place in (pltpu.VMEM, pltpu.VMEM, pltpu.HBM))


def call(kernel, products, ins, outs, scratch, copies):
    def shape_of(place, shape, dtype):
        if place is HB:
            return pltpu.HBM(shape, dtype)
        if place is PV:
            return pltpu.VMEM(shape, dtype)
        return jax.ShapeDtypeStruct(shape, dtype)

    run = pl.pallas_call(
        kernel,
        out_shape=[shape_of(*out) for out in outs],
        in_specs=ins,
        out_specs=[out[0] for out in outs],
        scratch_shapes=[pltpu.VMEM(shape, dtype) for shape, dtype in scratch]
        + ([pltpu.SemaphoreType.DMA((copies,))] if copies else []),
        compiler_params=pltpu.CompilerParams(vmem_limit_bytes=28 << 20),
        cost_estimate=pl.CostEstimate(
            flops=products * 12 * 256 * 256 * 1024, bytes_accessed=4 << 20, transcendentals=1 << 18
        ),
    )

    def pinned(*values):
        return run(
            *[pltpu.with_memory_space_constraint(v, pltpu.HBM) if spec is HB else v for v, spec in zip(values, ins)]
        )

    return pinned


def on_device(image_embeds, text_embeds):
    images, texts = image_embeds[0, 0], text_embeds[0, 0]
    count, width = images.shape
    small = width // 4
    square, row, whole = ((count, count), f32), ((1, count), f32), ((count, width), f32)
    parts, left = ((3, count, width), bf16), ((count, len(PAIRS) * count), bf16)
    devices = lax.axis_size("dp") * lax.axis_size("hst")
    earlier_texts = from_behind(texts, "dp", 1)
    (
        image_parts, self_rows, self_columns, first, second, logits, image_store, text_store, row_product, column_term
    ) = call(
        self_kernel,
        3,
        [HB, HB],
        [
            (VM, *parts), (VM, *row), (VM, (2, count), f32),
            (PV, (count, width - small), f32), (PV, (count, small), f32), (HB, *square), (HB, *parts), (HB, *parts), (HB, *whole), (HB, *whole),
        ],
        [square, whole, whole, parts, left, left, whole, whole],
        6,
    )(images, texts)
    before_columns = from_behind(self_columns, "dp", 1)
    later_rows = from_behind(self_rows, "dp", -1)
    earlier_texts, first, second, before_columns, later_rows, image_parts = lax.optimization_barrier(
        (earlier_texts, first, second, before_columns, later_rows, image_parts)
    )
    first = from_behind(first, "dp", -1)
    messages, weights, rows = call(
        earlier_kernel,
        1,
        [VM] * 5,
        [(HB, (devices, 1, LANES), f32), (VM, *square), (VM, *row)],
        [((devices, 1, LANES), f32)],
        1,
    )(image_parts, earlier_texts, self_rows, self_columns, before_columns)
    second, weights = lax.optimization_barrier((second, weights))
    second = from_behind(second, "dp", -1)
    messages = lax.all_to_all(messages, ("dp", "hst"), 0, 0, tiled=True)
    image_part, row_term, text_parts, logits = call(
        middle_kernel,
        2,
        [VM] * 4 + [HB] * 4,
        [(VM, *whole), (VM, *whole), (VM, *parts), (VM, *square)],
        [parts, parts, whole, left, left],
        4,
    )(weights, earlier_texts, rows, self_rows, logits, image_store, text_store, row_product)
    first_parts, product, column_term, images = call(
        first_kernel,
        1,
        [VM, VM, HB, HB],
        [(VM, (3, count, width - small), bf16), (VM, *square), (VM, *whole), (VM, *whole)],
        [],
        2,
    )(text_parts, first, column_term, images)
    image_grads, text_grads = call(
        last_kernel,
        3,
        [VM] * 12,
        [(HB, *whole), (HB, *whole)],
        [parts, left, left, whole, whole],
        4,
    )(
        text_parts, first_parts, second, product, logits, rows, later_rows, self_columns, image_part, row_term, column_term, images
    )
    messages, text_grads = lax.optimization_barrier((messages, text_grads))
    (mean_loss,) = call(functools.partial(loss_kernel, rows=count * devices), 0, [VM], [(VM, (1, 1), f32)], [], 0)(messages)
    return mean_loss[0, 0], image_grads[None, None], text_grads[None, None]


def solution(mesh):
    return jax.shard_map(
        on_device,
        mesh=mesh,
        in_specs=(P("dp", "hst", None, None), P("dp", "hst", None, None)),
        out_specs=(P(), P("dp", "hst", None, None), P("dp", "hst", None, None)),
        check_vma=False,
    )
```

```python
import functools

import jax
import jax.numpy as jnp
from jax import lax
from jax.experimental import pallas as pl
from jax.experimental.pallas import tpu as pltpu
from jax.sharding import PartitionSpec as P

logit_scale = 0.03125
f32, bf16 = jnp.float32, jnp.bfloat16
LANES = 128


def from_behind(value, axis, steps):
    count = lax.axis_size(axis)
    pairs = [(source, (source + steps) % count) for source in range(count)]
    return lax.ppermute(value, axis, pairs)


def split(value):
    high = value.astype(bf16)
    rest = value - high.astype(f32)
    middle = rest.astype(bf16)
    low = (rest - middle.astype(f32)).astype(bf16)
    return high, middle, low


PAIRS = ((2, 0), (1, 1), (0, 2), (1, 0), (0, 1), (0, 0))


def rows_by_rows(left, right):
    return lax.dot_general(
        jnp.concatenate([left[one] for one, _ in PAIRS], axis=1),
        jnp.concatenate([right[other] for _, other in PAIRS], axis=1),
        (((1,), (1,)), ((), ())),
        preferred_element_type=f32,
    )


def left_parts(left):
    parts = split(left)
    return jnp.concatenate([parts[one] for one, _ in PAIRS], axis=1)


def rows_by_columns(left, right):
    return jnp.dot(left, jnp.concatenate([right[other] for _, other in PAIRS], axis=0), preferred_element_type=f32)


def store_parts(stacked, value):
    for place, part in enumerate(split(value)):
        stacked[place] = part


def logsum(logits, axis):
    largest = jnp.max(logits, axis=axis, keepdims=True)
    return largest + jnp.log(jnp.sum(jnp.exp(logits - largest), axis=axis, keepdims=True))


def paired_logsum(former, latter):
    largest = jnp.maximum(former, latter)
    return largest + jnp.log(jnp.exp(former - largest) + jnp.exp(latter - largest))


def joint_logsum(logits, other, axis):
    largest = jnp.max(logits, axis=axis, keepdims=True)
    powers = jnp.exp(logits - largest)
    joint = paired_logsum(other, largest + jnp.log(jnp.sum(powers, axis=axis, keepdims=True)))
    return joint, powers * (0.5 * jnp.exp(largest - joint))


def diagonal_mask(count):
    shape = (count, count)
    return lax.broadcasted_iota(jnp.int32, shape, 0) == lax.broadcasted_iota(jnp.int32, shape, 1)


def as_row(column, diagonal):
    return jnp.sum(jnp.where(diagonal, column, 0.0), axis=0, keepdims=True)


def as_column(row, diagonal):
    return jnp.sum(jnp.where(diagonal, row, 0.0), axis=1, keepdims=True)


def total(values):
    return jnp.sum(jnp.sum(values, axis=1, keepdims=True), axis=0, keepdims=True)


def start(pairs, semaphores):
    copies = [pltpu.make_async_copy(source, target, semaphores.at[k]) for k, (source, target) in enumerate(pairs)]
    for copy in copies:
        copy.start()
    return copies


def columns_at(k, size):
    return pl.ds(pl.multiple_of(k * size, size), size)


def self_kernel(
    images, texts,
    image_parts, row_part, columns_out, first, second, logits, text_store, row_product, column_term,
    own, image_in, text_in, text_parts, left, down, row_out, column_out, semaphores,
):
    copies = start([(images, image_in), (texts, text_in)], semaphores)
    copies[0].wait()
    store_parts(image_parts, image_in[...])
    border = first.shape[1]
    first[...] = image_in[:, :border]
    second[...] = image_in[:, border:]
    copies[1].wait()
    store_parts(text_parts, text_in[...])
    copies = start([(text_parts, text_store)], semaphores)
    block = logit_scale * rows_by_rows(image_parts, text_parts)
    count, width = text_in.shape
    diagonal = diagonal_mask(count)
    rows, columns = logsum(block, 1), logsum(block, 0)
    own[...] = block
    row_part[...] = as_row(rows, diagonal)
    columns_out[0:1, :] = columns
    columns_out[1:2, :] = as_row(block, diagonal)
    left[...] = left_parts(jnp.where(diagonal, 0.0, 0.5 * jnp.exp(block - rows)))
    down[...] = left_parts(jnp.where(diagonal, 0.0, 0.5 * jnp.exp(block - columns)).T)
    half = width // 2

    @pl.loop(0, 2)
    def _(k):
        part = columns_at(k, half)
        row_out[:, part] = rows_by_columns(left[...], text_parts.at[:, :, part])
        column_out[:, part] = rows_by_columns(down[...], image_parts.at[:, :, part])

    copies += start([(row_out, row_product), (column_out, column_term), (own, logits)], semaphores.at[1:4])
    for copy in copies:
        copy.wait()


def earlier_kernel(
    image_parts, earlier_texts, self_rows, self_columns, before_columns,
    messages, weights, rows_out,
    letters, semaphores,
):
    block = logit_scale * rows_by_rows(image_parts, split(earlier_texts[...]))
    diagonal = diagonal_mask(block.shape[0])
    rows = paired_logsum(self_rows[...], as_row(logsum(block, 1), diagonal))
    columns = paired_logsum(before_columns[0:1, :], logsum(block, 0))
    partial = 0.5 * jnp.sum((rows - self_columns[1:2, :]) + (columns - before_columns[1:2, :]), axis=1, keepdims=True)
    letters[...] = jnp.broadcast_to(partial, letters.shape)
    (copy,) = start([(letters, messages)], semaphores)
    weights[...] = 0.5 * (jnp.exp(block - as_column(rows, diagonal)) + jnp.exp(block - columns))
    rows_out[...] = rows
    copy.wait()


def middle_kernel(
    weights, earlier_texts, rows, self_rows, logits, images, text_store, row_store,
    image_part, row_term, text_parts, own, own_images,
    earlier_parts, image_parts, row_product, left, down, semaphores,
):
    copies = start(
        [(logits, own), (images, own_images), (row_store, row_product), (text_store, text_parts)], semaphores
    )
    count, width = image_part.shape
    diagonal = diagonal_mask(count)
    left[...] = left_parts(weights[...])
    store_parts(earlier_parts, earlier_texts[...])
    joint = as_column(rows[...], diagonal)
    scale = as_column(jnp.exp(self_rows[...] - rows[...]), diagonal)
    half = width // 2

    @pl.loop(0, 2)
    def _(k):
        part = columns_at(k, half)
        image_part[:, part] = rows_by_columns(left[...], earlier_parts.at[:, :, part])

    copies[0].wait()
    down[...] = left_parts(jnp.where(diagonal, 0.0, 0.5 * jnp.exp(own[...] - joint)).T)
    copies[1].wait()
    store_parts(image_parts, own_images[...])

    @pl.loop(0, 2)
    def _(k):
        part = columns_at(k, half)
        row_term[:, part] = rows_by_columns(down[...], image_parts.at[:, :, part])

    copies[2].wait()
    image_part[...] += scale * row_product[...]
    copies[3].wait()


def first_kernel(text_parts, first, column_store, first_parts, product, column_term, semaphores):
    (copy,) = start([(column_store, column_term)], semaphores)
    store_parts(first_parts, first[...])
    product[...] = rows_by_rows(text_parts.at[:, :, : first.shape[1]], first_parts)
    copy.wait()


def last_kernel(
    text_parts, first_parts, second, product, logits, rows_in, later_rows, self_columns, image_part, row_term, column_term, image_in,
    image_grads, text_grads,
    later_parts, left, own_left, image_out, text_out, semaphores,
):
    count, width = image_out.shape
    diagonal = diagonal_mask(count)
    border = first_parts.shape[2]
    part = slice(border, width)
    later_parts[:, :, :border] = first_parts[...]
    store_parts(later_parts.at[:, :, part], second[...])
    block = logit_scale * (product[...] + rows_by_rows(text_parts.at[:, :, part], later_parts.at[:, :, part]))
    own_columns = as_column(self_columns[0:1, :], diagonal)
    rows, by_rows = joint_logsum(block, later_rows[...], 0)
    columns, by_columns = joint_logsum(block, own_columns, 1)
    left[...] = left_parts(by_rows + by_columns)
    across, positive = as_row(columns, diagonal), self_columns[1:2, :]
    own = 0.5 * (jnp.exp(positive - rows_in[...]) + jnp.exp(positive - across)) - 1.0
    own_left[...] = left_parts(jnp.where(diagonal, own, 0.5 * jnp.exp(logits[...] - across)))
    own_down = as_column(own, diagonal)
    scale = jnp.exp(own_columns - columns)
    half = width // 2

    def copies(k):
        part = columns_at(k, half)
        return (
            pltpu.make_async_copy(image_out.at[:, part], image_grads.at[:, part], semaphores.at[2 * k]),
            pltpu.make_async_copy(text_out.at[:, part], text_grads.at[:, part], semaphores.at[2 * k + 1]),
        )

    @pl.loop(0, 2)
    def _(k):
        part = columns_at(k, half)
        of_image, of_text = copies(k)
        terms = rows_by_columns(own_left[...], text_parts.at[:, :, part])
        image_out[:, part] = logit_scale * (image_part[:, part] + terms)
        of_image.start()
        terms = rows_by_columns(left[...], later_parts.at[:, :, part])
        own_terms = row_term[:, part] + scale * column_term[:, part] + own_down * image_in[:, part]
        text_out[:, part] = logit_scale * (own_terms + terms)
        of_text.start()

    for k in range(2):
        for copy in copies(k):
            copy.wait()


def loss_kernel(messages, mean_loss, *, rows):
    mean_loss[...] = total(messages[:, 0, 0:1]) / rows


VM, PV, HB = (pl.BlockSpec(memory_space=place) for place in (pltpu.VMEM, pltpu.VMEM, pltpu.HBM))


def call(kernel, products, ins, outs, scratch, copies):
    def shape_of(place, shape, dtype):
        if place is HB:
            return pltpu.HBM(shape, dtype)
        if place is PV:
            return pltpu.VMEM(shape, dtype)
        return jax.ShapeDtypeStruct(shape, dtype)

    run = pl.pallas_call(
        kernel,
        out_shape=[shape_of(*out) for out in outs],
        in_specs=ins,
        out_specs=[out[0] for out in outs],
        scratch_shapes=[pltpu.VMEM(shape, dtype) for shape, dtype in scratch]
        + ([pltpu.SemaphoreType.DMA((copies,))] if copies else []),
        compiler_params=pltpu.CompilerParams(vmem_limit_bytes=28 << 20),
        cost_estimate=pl.CostEstimate(
            flops=products * 12 * 256 * 256 * 1024, bytes_accessed=4 << 20, transcendentals=1 << 18
        ),
    )

    def pinned(*values):
        return run(
            *[pltpu.with_memory_space_constraint(v, pltpu.HBM) if spec is HB else v for v, spec in zip(values, ins)]
        )

    return pinned


def on_device(image_embeds, text_embeds):
    images, texts = image_embeds[0, 0], text_embeds[0, 0]
    count, width = images.shape
    small = width // 4
    square, row, whole = ((count, count), f32), ((1, count), f32), ((count, width), f32)
    parts, left = ((3, count, width), bf16), ((count, len(PAIRS) * count), bf16)
    devices = lax.axis_size("dp") * lax.axis_size("hst")
    earlier_texts = from_behind(texts, "dp", 1)
    (
        image_parts, self_rows, self_columns, first, second, logits, text_store, row_product, column_term
    ) = call(
        self_kernel,
        3,
        [HB, HB],
        [
            (VM, *parts), (VM, *row), (VM, (2, count), f32),
            (PV, (count, width - small), f32), (PV, (count, small), f32), (HB, *square), (HB, *parts), (HB, *whole), (HB, *whole),
        ],
        [square, whole, whole, parts, left, left, whole, whole],
        4,
    )(images, texts)
    before_columns = from_behind(self_columns, "dp", 1)
    later_rows = from_behind(self_rows, "dp", -1)
    earlier_texts, first, second, before_columns, later_rows, image_parts = lax.optimization_barrier(
        (earlier_texts, first, second, before_columns, later_rows, image_parts)
    )
    first = from_behind(first, "dp", -1)
    messages, weights, rows = call(
        earlier_kernel,
        1,
        [VM] * 5,
        [(HB, (devices, 1, LANES), f32), (VM, *square), (VM, *row)],
        [((devices, 1, LANES), f32)],
        1,
    )(image_parts, earlier_texts, self_rows, self_columns, before_columns)
    second, weights = lax.optimization_barrier((second, weights))
    second = from_behind(second, "dp", -1)
    messages = lax.all_to_all(messages, ("dp", "hst"), 0, 0, tiled=True)
    image_part, row_term, text_parts, logits, own_images = call(
        middle_kernel,
        2,
        [VM] * 4 + [HB] * 4,
        [(VM, *whole), (VM, *whole), (VM, *parts), (VM, *square), (VM, *whole)],
        [parts, parts, whole, left, left],
        4,
    )(weights, earlier_texts, rows, self_rows, logits, images, text_store, row_product)
    first_parts, product, column_term = call(
        first_kernel,
        1,
        [VM, VM, HB],
        [(VM, (3, count, width - small), bf16), (VM, *square), (VM, *whole)],
        [],
        1,
    )(text_parts, first, column_term)
    image_grads, text_grads = call(
        last_kernel,
        3,
        [VM] * 12,
        [(HB, *whole), (HB, *whole)],
        [parts, left, left, whole, whole],
        4,
    )(
        text_parts, first_parts, second, product, logits, rows, later_rows, self_columns, image_part, row_term, column_term, own_images
    )
    messages, text_grads = lax.optimization_barrier((messages, text_grads))
    (mean_loss,) = call(functools.partial(loss_kernel, rows=count * devices), 0, [VM], [(VM, (1, 1), f32)], [], 0)(messages)
    return mean_loss[0, 0], image_grads[None, None], text_grads[None, None]


def solution(mesh):
    return jax.shard_map(
        on_device,
        mesh=mesh,
        in_specs=(P("dp", "hst", None, None), P("dp", "hst", None, None)),
        out_specs=(P(), P("dp", "hst", None, None), P("dp", "hst", None, None)),
        check_vma=False,
    )
```

```python
import functools

import jax
import jax.numpy as jnp
from jax import lax
from jax.experimental import pallas as pl
from jax.experimental.pallas import tpu as pltpu
from jax.sharding import PartitionSpec as P

logit_scale = 0.03125
f32, bf16 = jnp.float32, jnp.bfloat16
LANES = 128


def from_behind(value, axis, steps):
    count = lax.axis_size(axis)
    pairs = [(source, (source + steps) % count) for source in range(count)]
    return lax.ppermute(value, axis, pairs)


def split(value):
    high = value.astype(bf16)
    rest = value - high.astype(f32)
    middle = rest.astype(bf16)
    low = (rest - middle.astype(f32)).astype(bf16)
    return high, middle, low


PAIRS = ((2, 0), (1, 1), (0, 2), (1, 0), (0, 1), (0, 0))


def rows_by_rows(left, right):
    return lax.dot_general(
        jnp.concatenate([left[one] for one, _ in PAIRS], axis=1),
        jnp.concatenate([right[other] for _, other in PAIRS], axis=1),
        (((1,), (1,)), ((), ())),
        preferred_element_type=f32,
    )


def left_parts(left):
    parts = split(left)
    return jnp.concatenate([parts[one] for one, _ in PAIRS], axis=1)


def rows_by_columns(left, right):
    return jnp.dot(left, jnp.concatenate([right[other] for _, other in PAIRS], axis=0), preferred_element_type=f32)


def store_parts(stacked, value):
    for place, part in enumerate(split(value)):
        stacked[place] = part


def logsum(logits, axis):
    largest = jnp.max(logits, axis=axis, keepdims=True)
    return largest + jnp.log(jnp.sum(jnp.exp(logits - largest), axis=axis, keepdims=True))


def paired_logsum(former, latter):
    largest = jnp.maximum(former, latter)
    return largest + jnp.log(jnp.exp(former - largest) + jnp.exp(latter - largest))


def joint_logsum(logits, other, axis):
    largest = jnp.max(logits, axis=axis, keepdims=True)
    powers = jnp.exp(logits - largest)
    joint = paired_logsum(other, largest + jnp.log(jnp.sum(powers, axis=axis, keepdims=True)))
    return joint, powers * (0.5 * jnp.exp(largest - joint))


def diagonal_mask(count):
    shape = (count, count)
    return lax.broadcasted_iota(jnp.int32, shape, 0) == lax.broadcasted_iota(jnp.int32, shape, 1)


def as_row(column, diagonal):
    return jnp.sum(jnp.where(diagonal, column, 0.0), axis=0, keepdims=True)


def as_column(row, diagonal):
    return jnp.sum(jnp.where(diagonal, row, 0.0), axis=1, keepdims=True)


def total(values):
    return jnp.sum(jnp.sum(values, axis=1, keepdims=True), axis=0, keepdims=True)


def start(pairs, semaphores):
    copies = [pltpu.make_async_copy(source, target, semaphores.at[k]) for k, (source, target) in enumerate(pairs)]
    for copy in copies:
        copy.start()
    return copies


def columns_at(k, size):
    return pl.ds(pl.multiple_of(k * size, size), size)


def self_kernel(
    images, texts,
    image_parts, row_part, columns_out, first, second, logits, text_store, row_product, column_term,
    own, image_in, text_in, text_parts, left, down, row_out, column_out, semaphores,
):
    copies = start([(images, image_in), (texts, text_in)], semaphores)
    copies[0].wait()
    store_parts(image_parts, image_in[...])
    border = first.shape[1]
    first[...] = image_in[:, :border]
    second[...] = image_in[:, border:]
    copies[1].wait()
    store_parts(text_parts, text_in[...])
    copies = start([(text_parts, text_store)], semaphores)
    block = logit_scale * rows_by_rows(image_parts, text_parts)
    count, width = text_in.shape
    diagonal = diagonal_mask(count)
    rows, columns = logsum(block, 1), logsum(block, 0)
    own[...] = block
    row_part[...] = as_row(rows, diagonal)
    columns_out[0:1, :] = columns
    columns_out[1:2, :] = as_row(block, diagonal)
    left[...] = left_parts(jnp.where(diagonal, 0.0, 0.5 * jnp.exp(block - rows)))
    down[...] = left_parts(jnp.where(diagonal, 0.0, 0.5 * jnp.exp(block - columns)).T)
    half = width // 2

    @pl.loop(0, 2)
    def _(k):
        part = columns_at(k, half)
        row_out[:, part] = rows_by_columns(left[...], text_parts.at[:, :, part])
        column_out[:, part] = rows_by_columns(down[...], image_parts.at[:, :, part])

    copies += start([(row_out, row_product), (column_out, column_term), (own, logits)], semaphores.at[1:4])
    for copy in copies:
        copy.wait()


def earlier_kernel(
    image_parts, earlier_texts, self_rows, self_columns, before_columns,
    messages, weights, rows_out,
    letters, semaphores,
):
    block = logit_scale * rows_by_rows(image_parts, split(earlier_texts[...]))
    diagonal = diagonal_mask(block.shape[0])
    rows = paired_logsum(self_rows[...], as_row(logsum(block, 1), diagonal))
    columns = paired_logsum(before_columns[0:1, :], logsum(block, 0))
    partial = 0.5 * jnp.sum((rows - self_columns[1:2, :]) + (columns - before_columns[1:2, :]), axis=1, keepdims=True)
    letters[...] = jnp.broadcast_to(partial, letters.shape)
    (copy,) = start([(letters, messages)], semaphores)
    weights[...] = 0.5 * (jnp.exp(block - as_column(rows, diagonal)) + jnp.exp(block - columns))
    rows_out[...] = rows
    copy.wait()


def middle_kernel(
    weights, earlier_texts, rows, self_rows, logits, images, text_store, row_store,
    image_part, row_term, text_parts, own, own_images,
    earlier_parts, image_parts, row_product, left, down, semaphores,
):
    copies = start(
        [(logits, own), (images, own_images), (row_store, row_product), (text_store, text_parts)], semaphores
    )
    count, width = image_part.shape
    diagonal = diagonal_mask(count)
    left[...] = left_parts(weights[...])
    store_parts(earlier_parts, earlier_texts[...])
    joint = as_column(rows[...], diagonal)
    scale = as_column(jnp.exp(self_rows[...] - rows[...]), diagonal)
    half = width // 2

    @pl.loop(0, 2)
    def _(k):
        part = columns_at(k, half)
        image_part[:, part] = rows_by_columns(left[...], earlier_parts.at[:, :, part])

    copies[0].wait()
    down[...] = left_parts(jnp.where(diagonal, 0.0, 0.5 * jnp.exp(own[...] - joint)).T)
    copies[1].wait()
    store_parts(image_parts, own_images[...])

    @pl.loop(0, 2)
    def _(k):
        part = columns_at(k, half)
        row_term[:, part] = rows_by_columns(down[...], image_parts.at[:, :, part])

    copies[2].wait()
    image_part[...] += scale * row_product[...]
    copies[3].wait()


def first_kernel(text_parts, first, column_store, first_parts, product, column_term, semaphores):
    (copy,) = start([(column_store, column_term)], semaphores)
    store_parts(first_parts, first[...])
    product[...] = rows_by_rows(text_parts.at[:, :, : first.shape[1]], first_parts)
    copy.wait()


def last_kernel(
    text_parts, first_parts, second, product, logits, rows_in, later_rows, self_columns, image_part, row_term, column_term, image_in,
    image_grads, text_grads,
    later_parts, left, own_left, image_out, text_out, semaphores,
):
    count, width = image_out.shape
    diagonal = diagonal_mask(count)
    border = first_parts.shape[2]
    part = slice(border, width)
    later_parts[:, :, :border] = first_parts[...]
    store_parts(later_parts.at[:, :, part], second[...])
    block = logit_scale * (product[...] + rows_by_rows(text_parts.at[:, :, part], later_parts.at[:, :, part]))
    own_columns = as_column(self_columns[0:1, :], diagonal)
    rows, by_rows = joint_logsum(block, later_rows[...], 0)
    columns, by_columns = joint_logsum(block, own_columns, 1)
    left[...] = left_parts(by_rows + by_columns)
    across, positive = as_row(columns, diagonal), self_columns[1:2, :]
    own = 0.5 * (jnp.exp(positive - rows_in[...]) + jnp.exp(positive - across)) - 1.0
    own_left[...] = left_parts(jnp.where(diagonal, own, 0.5 * jnp.exp(logits[...] - across)))
    own_down = as_column(own, diagonal)
    scale = jnp.exp(own_columns - columns)
    half = width // 2

    def copies(k):
        part = columns_at(k, half)
        return (
            pltpu.make_async_copy(image_out.at[:, part], image_grads.at[:, part], semaphores.at[2 * k]),
            pltpu.make_async_copy(text_out.at[:, part], text_grads.at[:, part], semaphores.at[2 * k + 1]),
        )

    @pl.loop(0, 2, unroll=True)
    def _(k):
        part = columns_at(k, half)
        of_image, of_text = copies(k)
        terms = rows_by_columns(own_left[...], text_parts.at[:, :, part])
        image_out[:, part] = logit_scale * (image_part[:, part] + terms)
        of_image.start()
        terms = rows_by_columns(left[...], later_parts.at[:, :, part])
        own_terms = row_term[:, part] + scale * column_term[:, part] + own_down * image_in[:, part]
        text_out[:, part] = logit_scale * (own_terms + terms)
        of_text.start()

    for k in range(2):
        for copy in copies(k):
            copy.wait()


def loss_kernel(messages, mean_loss, *, rows):
    mean_loss[...] = total(messages[:, 0, 0:1]) / rows


VM, PV, HB = (pl.BlockSpec(memory_space=place) for place in (pltpu.VMEM, pltpu.VMEM, pltpu.HBM))


def call(kernel, products, ins, outs, scratch, copies):
    def shape_of(place, shape, dtype):
        if place is HB:
            return pltpu.HBM(shape, dtype)
        if place is PV:
            return pltpu.VMEM(shape, dtype)
        return jax.ShapeDtypeStruct(shape, dtype)

    run = pl.pallas_call(
        kernel,
        out_shape=[shape_of(*out) for out in outs],
        in_specs=ins,
        out_specs=[out[0] for out in outs],
        scratch_shapes=[pltpu.VMEM(shape, dtype) for shape, dtype in scratch]
        + ([pltpu.SemaphoreType.DMA((copies,))] if copies else []),
        compiler_params=pltpu.CompilerParams(vmem_limit_bytes=28 << 20),
        cost_estimate=pl.CostEstimate(
            flops=products * 12 * 256 * 256 * 1024, bytes_accessed=4 << 20, transcendentals=1 << 18
        ),
    )

    def pinned(*values):
        return run(
            *[pltpu.with_memory_space_constraint(v, pltpu.HBM) if spec is HB else v for v, spec in zip(values, ins)]
        )

    return pinned


def on_device(image_embeds, text_embeds):
    images, texts = image_embeds[0, 0], text_embeds[0, 0]
    count, width = images.shape
    small = width // 4
    square, row, whole = ((count, count), f32), ((1, count), f32), ((count, width), f32)
    parts, left = ((3, count, width), bf16), ((count, len(PAIRS) * count), bf16)
    devices = lax.axis_size("dp") * lax.axis_size("hst")
    earlier_texts = from_behind(texts, "dp", 1)
    (
        image_parts, self_rows, self_columns, first, second, logits, text_store, row_product, column_term
    ) = call(
        self_kernel,
        3,
        [HB, HB],
        [
            (VM, *parts), (VM, *row), (VM, (2, count), f32),
            (PV, (count, width - small), f32), (PV, (count, small), f32), (HB, *square), (HB, *parts), (HB, *whole), (HB, *whole),
        ],
        [square, whole, whole, parts, left, left, whole, whole],
        4,
    )(images, texts)
    before_columns = from_behind(self_columns, "dp", 1)
    later_rows = from_behind(self_rows, "dp", -1)
    earlier_texts, first, second, before_columns, later_rows, image_parts = lax.optimization_barrier(
        (earlier_texts, first, second, before_columns, later_rows, image_parts)
    )
    first = from_behind(first, "dp", -1)
    messages, weights, rows = call(
        earlier_kernel,
        1,
        [VM] * 5,
        [(HB, (devices, 1, LANES), f32), (VM, *square), (VM, *row)],
        [((devices, 1, LANES), f32)],
        1,
    )(image_parts, earlier_texts, self_rows, self_columns, before_columns)
    second, weights = lax.optimization_barrier((second, weights))
    second = from_behind(second, "dp", -1)
    messages = lax.all_to_all(messages, ("dp", "hst"), 0, 0, tiled=True)
    image_part, row_term, text_parts, logits, own_images = call(
        middle_kernel,
        2,
        [VM] * 4 + [HB] * 4,
        [(VM, *whole), (VM, *whole), (VM, *parts), (VM, *square), (VM, *whole)],
        [parts, parts, whole, left, left],
        4,
    )(weights, earlier_texts, rows, self_rows, logits, images, text_store, row_product)
    first_parts, product, column_term = call(
        first_kernel,
        1,
        [VM, VM, HB],
        [(VM, (3, count, width - small), bf16), (VM, *square), (VM, *whole)],
        [],
        1,
    )(text_parts, first, column_term)
    image_grads, text_grads = call(
        last_kernel,
        3,
        [VM] * 12,
        [(HB, *whole), (HB, *whole)],
        [parts, left, left, whole, whole],
        4,
    )(
        text_parts, first_parts, second, product, logits, rows, later_rows, self_columns, image_part, row_term, column_term, own_images
    )
    messages, text_grads = lax.optimization_barrier((messages, text_grads))
    (mean_loss,) = call(functools.partial(loss_kernel, rows=count * devices), 0, [VM], [(VM, (1, 1), f32)], [], 0)(messages)
    return mean_loss[0, 0], image_grads[None, None], text_grads[None, None]


def solution(mesh):
    return jax.shard_map(
        on_device,
        mesh=mesh,
        in_specs=(P("dp", "hst", None, None), P("dp", "hst", None, None)),
        out_specs=(P(), P("dp", "hst", None, None), P("dp", "hst", None, None)),
        check_vma=False,
    )
```

```python
import functools

import jax
import jax.numpy as jnp
from jax import lax
from jax.experimental import pallas as pl
from jax.experimental.pallas import tpu as pltpu
from jax.sharding import PartitionSpec as P

logit_scale = 0.03125
f32, bf16 = jnp.float32, jnp.bfloat16
LANES = 128


def from_behind(value, axis, steps):
    count = lax.axis_size(axis)
    pairs = [(source, (source + steps) % count) for source in range(count)]
    return lax.ppermute(value, axis, pairs)


def split(value):
    high = value.astype(bf16)
    rest = value - high.astype(f32)
    middle = rest.astype(bf16)
    low = (rest - middle.astype(f32)).astype(bf16)
    return high, middle, low


PAIRS = ((2, 0), (1, 1), (0, 2), (1, 0), (0, 1), (0, 0))


def rows_by_rows(left, right):
    return lax.dot_general(
        jnp.concatenate([left[one] for one, _ in PAIRS], axis=1),
        jnp.concatenate([right[other] for _, other in PAIRS], axis=1),
        (((1,), (1,)), ((), ())),
        preferred_element_type=f32,
    )


def left_parts(left):
    parts = split(left)
    return jnp.concatenate([parts[one] for one, _ in PAIRS], axis=1)


def rows_by_columns(left, right):
    return jnp.dot(left, jnp.concatenate([right[other] for _, other in PAIRS], axis=0), preferred_element_type=f32)


def store_parts(stacked, value):
    for place, part in enumerate(split(value)):
        stacked[place] = part


def logsum(logits, axis):
    largest = jnp.max(logits, axis=axis, keepdims=True)
    return largest + jnp.log(jnp.sum(jnp.exp(logits - largest), axis=axis, keepdims=True))


def paired_logsum(former, latter):
    largest = jnp.maximum(former, latter)
    return largest + jnp.log(jnp.exp(former - largest) + jnp.exp(latter - largest))


def joint_logsum(logits, other, axis):
    largest = jnp.max(logits, axis=axis, keepdims=True)
    powers = jnp.exp(logits - largest)
    joint = paired_logsum(other, largest + jnp.log(jnp.sum(powers, axis=axis, keepdims=True)))
    return joint, powers * (0.5 * jnp.exp(largest - joint))


def diagonal_mask(count):
    shape = (count, count)
    return lax.broadcasted_iota(jnp.int32, shape, 0) == lax.broadcasted_iota(jnp.int32, shape, 1)


def as_row(column, diagonal):
    return jnp.sum(jnp.where(diagonal, column, 0.0), axis=0, keepdims=True)


def as_column(row, diagonal):
    return jnp.sum(jnp.where(diagonal, row, 0.0), axis=1, keepdims=True)


def total(values):
    return jnp.sum(jnp.sum(values, axis=1, keepdims=True), axis=0, keepdims=True)


def start(pairs, semaphores):
    copies = [pltpu.make_async_copy(source, target, semaphores.at[k]) for k, (source, target) in enumerate(pairs)]
    for copy in copies:
        copy.start()
    return copies


def columns_at(k, size):
    return pl.ds(pl.multiple_of(k * size, size), size)


def self_kernel(
    images, texts,
    image_parts, row_part, columns_out, first, second, logits, text_store, row_product, column_term,
    own, image_in, text_in, text_parts, left, down, row_out, column_out, semaphores,
):
    copies = start([(images, image_in), (texts, text_in)], semaphores)
    copies[0].wait()
    store_parts(image_parts, image_in[...])
    border = first.shape[1]
    first[...] = image_in[:, :border]
    second[...] = image_in[:, border:]
    copies[1].wait()
    store_parts(text_parts, text_in[...])
    copies = start([(text_parts, text_store)], semaphores)
    block = logit_scale * rows_by_rows(image_parts, text_parts)
    count, width = text_in.shape
    diagonal = diagonal_mask(count)
    rows, columns = logsum(block, 1), logsum(block, 0)
    own[...] = block
    row_part[...] = as_row(rows, diagonal)
    columns_out[0:1, :] = columns
    columns_out[1:2, :] = as_row(block, diagonal)
    left[...] = left_parts(jnp.where(diagonal, 0.0, 0.5 * jnp.exp(block - rows)))
    down[...] = left_parts(jnp.where(diagonal, 0.0, 0.5 * jnp.exp(block - columns)).T)
    half = width // 2

    @pl.loop(0, 2)
    def _(k):
        part = columns_at(k, half)
        row_out[:, part] = rows_by_columns(left[...], text_parts.at[:, :, part])
        column_out[:, part] = rows_by_columns(down[...], image_parts.at[:, :, part])

    copies += start([(row_out, row_product), (column_out, column_term), (own, logits)], semaphores.at[1:4])
    for copy in copies:
        copy.wait()


def earlier_kernel(
    image_parts, earlier_texts, self_rows, self_columns, before_columns,
    messages, weights, rows_out,
    letters, semaphores,
):
    block = logit_scale * rows_by_rows(image_parts, split(earlier_texts[...]))
    diagonal = diagonal_mask(block.shape[0])
    rows = paired_logsum(self_rows[...], as_row(logsum(block, 1), diagonal))
    columns = paired_logsum(before_columns[0:1, :], logsum(block, 0))
    partial = 0.5 * jnp.sum((rows - self_columns[1:2, :]) + (columns - before_columns[1:2, :]), axis=1, keepdims=True)
    letters[...] = jnp.broadcast_to(partial, letters.shape)
    (copy,) = start([(letters, messages)], semaphores)
    weights[...] = 0.5 * (jnp.exp(block - as_column(rows, diagonal)) + jnp.exp(block - columns))
    rows_out[...] = rows
    copy.wait()


def middle_kernel(
    weights, earlier_texts, rows, self_rows, logits, images, text_store, row_store,
    image_part, row_term, text_parts, own, own_images,
    earlier_parts, image_parts, row_product, left, down, semaphores,
):
    copies = start(
        [(logits, own), (images, own_images), (row_store, row_product), (text_store, text_parts)], semaphores
    )
    count, width = image_part.shape
    diagonal = diagonal_mask(count)
    left[...] = left_parts(logit_scale * weights[...])
    store_parts(earlier_parts, earlier_texts[...])
    joint = as_column(rows[...], diagonal)
    scale = as_column(jnp.exp(self_rows[...] - rows[...]), diagonal)
    half = width // 2

    @pl.loop(0, 2)
    def _(k):
        part = columns_at(k, half)
        image_part[:, part] = rows_by_columns(left[...], earlier_parts.at[:, :, part])

    copies[0].wait()
    down[...] = left_parts(jnp.where(diagonal, 0.0, (0.5 * logit_scale) * jnp.exp(own[...] - joint)).T)
    copies[1].wait()
    store_parts(image_parts, own_images[...])

    @pl.loop(0, 2)
    def _(k):
        part = columns_at(k, half)
        row_term[:, part] = rows_by_columns(down[...], image_parts.at[:, :, part])

    copies[2].wait()
    image_part[...] += (logit_scale * scale) * row_product[...]
    copies[3].wait()


def first_kernel(text_parts, first, column_store, first_parts, product, column_term, semaphores):
    (copy,) = start([(column_store, column_term)], semaphores)
    store_parts(first_parts, first[...])
    product[...] = rows_by_rows(text_parts.at[:, :, : first.shape[1]], first_parts)
    copy.wait()


def last_kernel(
    text_parts, first_parts, second, product, logits, rows_in, later_rows, self_columns, image_part, row_term, column_term, image_in,
    image_grads, text_grads,
    later_parts, left, own_left, image_out, text_out, semaphores,
):
    count, width = image_out.shape
    diagonal = diagonal_mask(count)
    border = first_parts.shape[2]
    part = slice(border, width)
    later_parts[:, :, :border] = first_parts[...]
    store_parts(later_parts.at[:, :, part], second[...])
    block = logit_scale * (product[...] + rows_by_rows(text_parts.at[:, :, part], later_parts.at[:, :, part]))
    own_columns = as_column(self_columns[0:1, :], diagonal)
    rows, by_rows = joint_logsum(block, later_rows[...], 0)
    columns, by_columns = joint_logsum(block, own_columns, 1)
    left[...] = left_parts(logit_scale * (by_rows + by_columns))
    across, positive = as_row(columns, diagonal), self_columns[1:2, :]
    own = 0.5 * (jnp.exp(positive - rows_in[...]) + jnp.exp(positive - across)) - 1.0
    own_left[...] = left_parts(logit_scale * jnp.where(diagonal, own, 0.5 * jnp.exp(logits[...] - across)))
    own_down = logit_scale * as_column(own, diagonal)
    scale = logit_scale * jnp.exp(own_columns - columns)
    half = width // 2

    def copies(k):
        part = columns_at(k, half)
        return (
            pltpu.make_async_copy(image_out.at[:, part], image_grads.at[:, part], semaphores.at[2 * k]),
            pltpu.make_async_copy(text_out.at[:, part], text_grads.at[:, part], semaphores.at[2 * k + 1]),
        )

    @pl.loop(0, 2, unroll=True)
    def _(k):
        part = columns_at(k, half)
        of_image, of_text = copies(k)
        terms = rows_by_columns(own_left[...], text_parts.at[:, :, part])
        image_out[:, part] = image_part[:, part] + terms
        of_image.start()
        terms = rows_by_columns(left[...], later_parts.at[:, :, part])
        own_terms = row_term[:, part] + scale * column_term[:, part] + own_down * image_in[:, part]
        text_out[:, part] = own_terms + terms
        of_text.start()

    for k in range(2):
        for copy in copies(k):
            copy.wait()


def loss_kernel(messages, mean_loss, *, rows):
    mean_loss[...] = total(messages[:, 0, 0:1]) / rows


VM, PV, HB = (pl.BlockSpec(memory_space=place) for place in (pltpu.VMEM, pltpu.VMEM, pltpu.HBM))


def call(kernel, products, ins, outs, scratch, copies):
    def shape_of(place, shape, dtype):
        if place is HB:
            return pltpu.HBM(shape, dtype)
        if place is PV:
            return pltpu.VMEM(shape, dtype)
        return jax.ShapeDtypeStruct(shape, dtype)

    run = pl.pallas_call(
        kernel,
        out_shape=[shape_of(*out) for out in outs],
        in_specs=ins,
        out_specs=[out[0] for out in outs],
        scratch_shapes=[pltpu.VMEM(shape, dtype) for shape, dtype in scratch]
        + ([pltpu.SemaphoreType.DMA((copies,))] if copies else []),
        compiler_params=pltpu.CompilerParams(vmem_limit_bytes=28 << 20),
        cost_estimate=pl.CostEstimate(
            flops=products * 12 * 256 * 256 * 1024, bytes_accessed=4 << 20, transcendentals=1 << 18
        ),
    )

    def pinned(*values):
        return run(
            *[pltpu.with_memory_space_constraint(v, pltpu.HBM) if spec is HB else v for v, spec in zip(values, ins)]
        )

    return pinned


def on_device(image_embeds, text_embeds):
    images, texts = image_embeds[0, 0], text_embeds[0, 0]
    count, width = images.shape
    small = width // 4
    square, row, whole = ((count, count), f32), ((1, count), f32), ((count, width), f32)
    parts, left = ((3, count, width), bf16), ((count, len(PAIRS) * count), bf16)
    devices = lax.axis_size("dp") * lax.axis_size("hst")
    earlier_texts = from_behind(texts, "dp", 1)
    (
        image_parts, self_rows, self_columns, first, second, logits, text_store, row_product, column_term
    ) = call(
        self_kernel,
        3,
        [HB, HB],
        [
            (VM, *parts), (VM, *row), (VM, (2, count), f32),
            (PV, (count, width - small), f32), (PV, (count, small), f32), (HB, *square), (HB, *parts), (HB, *whole), (HB, *whole),
        ],
        [square, whole, whole, parts, left, left, whole, whole],
        4,
    )(images, texts)
    before_columns = from_behind(self_columns, "dp", 1)
    later_rows = from_behind(self_rows, "dp", -1)
    earlier_texts, first, second, before_columns, later_rows, image_parts = lax.optimization_barrier(
        (earlier_texts, first, second, before_columns, later_rows, image_parts)
    )
    first = from_behind(first, "dp", -1)
    messages, weights, rows = call(
        earlier_kernel,
        1,
        [VM] * 5,
        [(HB, (devices, 1, LANES), f32), (VM, *square), (VM, *row)],
        [((devices, 1, LANES), f32)],
        1,
    )(image_parts, earlier_texts, self_rows, self_columns, before_columns)
    second, weights = lax.optimization_barrier((second, weights))
    second = from_behind(second, "dp", -1)
    messages = lax.all_to_all(messages, ("dp", "hst"), 0, 0, tiled=True)
    image_part, row_term, text_parts, logits, own_images = call(
        middle_kernel,
        2,
        [VM] * 4 + [HB] * 4,
        [(VM, *whole), (VM, *whole), (VM, *parts), (VM, *square), (VM, *whole)],
        [parts, parts, whole, left, left],
        4,
    )(weights, earlier_texts, rows, self_rows, logits, images, text_store, row_product)
    first_parts, product, column_term = call(
        first_kernel,
        1,
        [VM, VM, HB],
        [(VM, (3, count, width - small), bf16), (VM, *square), (VM, *whole)],
        [],
        1,
    )(text_parts, first, column_term)
    image_grads, text_grads = call(
        last_kernel,
        3,
        [VM] * 12,
        [(HB, *whole), (HB, *whole)],
        [parts, left, left, whole, whole],
        4,
    )(
        text_parts, first_parts, second, product, logits, rows, later_rows, self_columns, image_part, row_term, column_term, own_images
    )
    messages, text_grads = lax.optimization_barrier((messages, text_grads))
    (mean_loss,) = call(functools.partial(loss_kernel, rows=count * devices), 0, [VM], [(VM, (1, 1), f32)], [], 0)(messages)
    return mean_loss[0, 0], image_grads[None, None], text_grads[None, None]


def solution(mesh):
    return jax.shard_map(
        on_device,
        mesh=mesh,
        in_specs=(P("dp", "hst", None, None), P("dp", "hst", None, None)),
        out_specs=(P(), P("dp", "hst", None, None), P("dp", "hst", None, None)),
        check_vma=False,
    )
```
